512 devices in a mesh: src: 16 (over y_hi, x, core), dst: 32 (over z, y_lo).
Axes of the slice: x: 4, y: 8 (y_hi: 2, y_lo: 4; y = y_hi * 4 + y_lo), z: 8, core: 2. Of those that a mesh axis runs over, the one named last changes fastest.
Arguments:
- source_embedding_table: float32 [16, 32, 128, 384], P('src', 'dst'), may hold values from -1.75 to 1.75
- source_adagrad_state: float32 [16, 32, 128], P('src', 'dst'), may hold values from 0.001 to 0.1
- destination_embedding_table: float32 [16, 32, 128, 384], P('src', 'dst'), may hold values from -1.75 to 1.75
- destination_adagrad_state: float32 [16, 32, 128], P('src', 'dst'), may hold values from 0.001 to 0.1
- relations: float32 [2048, 384], replicated, may hold values from -6 to 6
- rel_state: float32 [2048], P(('src', 'dst')), may hold values from 0.001 to 0.1
- source_edge_rows: int32 [16, 32, 3, 256], P('src', 'dst'), may hold values from 0 to 127
- destination_edge_rows: int32 [16, 32, 3, 256], P('src', 'dst'), may hold values from 0 to 127
- edge_relation_index: int32 [16, 32, 3, 256], P('src', 'dst'), may hold values from 0 to 2047
- negative_block_rows: int32 [16, 32, 3, 2, 128], P('src', 'dst'), may hold values from 0 to 127
- bucket_block_counts: int32 [16, 32, 3], P('src', 'dst'), may hold values from 1 to 2
Outputs:
- src_out: float32 [16, 32, 128, 384], P('src', 'dst')
- src_state_out: float32 [16, 32, 128], P('src', 'dst')
- dst_out: float32 [16, 32, 128, 384], P('src', 'dst')
- dst_state_out: float32 [16, 32, 128], P('src', 'dst')
- rel_out: float32 [2048, 384], P(('src', 'dst'))
- rel_state_out: float32 [2048], P(('src', 'dst'))
The draws below stay inside these ranges and needn't reach their ends.
All inputs are finite; a program needn't handle non-finite values.
Results may differ from the reference program's by a relative error of at most 0.0004.
Values sent between devices are 32-bit elements; how exact they have to be, the bound alone decides.
A program may use at most 64 MiB of HBM per device.

```python
import math
import jax
import jax.numpy as jnp
from jax import lax

D = 384
NREL = 2048
ROWS = 128
EDGES = 256
NEG = 128
STEPS = 3
GROUPS = 2
N_SRC = 16
N_DST = 32


def draw_bucket_block_counts(key, part):
    key = jax.random.fold_in(key, 12)
    first, second = jax.random.split(key)
    counts = jax.random.randint(first, (N_SRC * N_DST * STEPS,), max(1, GROUPS // 4), GROUPS + 1)
    where_full = jax.random.randint(second, (), 0, N_SRC * N_DST * STEPS)
    counts = counts.at[where_full].set(GROUPS)
    return counts.reshape(N_SRC, N_DST, STEPS).astype(jnp.int32)


def plant(drawn, stream_key, low, top_value):
    longest = drawn.shape.index(max(drawn.shape))
    spots = []
    for shift in (0, 1):
        where = [jax.random.randint(jax.random.fold_in(stream_key, axis), (), 0, length) for axis, length in enumerate(drawn.shape)]
        where[longest] = (where[longest] + shift) % drawn.shape[longest]
        spots.append(tuple(where))
    return drawn.at[spots[0]].set(low).at[spots[1]].set(top_value)


def steps_of(rng, dims, cuts, low, high):
    level, own = 1.0, jax.random.fold_in(rng, 6)
    for axis_at, parts in cuts:
        draws = jnp.exp(jax.random.uniform(jax.random.fold_in(own, axis_at), (parts,), jnp.float32, low / len(cuts), high / len(cuts)))
        level = level * jnp.repeat(draws, dims[axis_at] // parts).reshape([-1 if axis == axis_at else 1 for axis in range(len(dims))])
    return level


def gaussian(own_key, dims, spread, most, shards=(), dtype=jnp.bfloat16):
    result = spread * jax.random.normal(own_key, dims, jnp.float32)
    if shards:
        result = result * steps_of(own_key, dims, shards, -0.22, 0.18)
    return jnp.clip(result, -most, most).astype(dtype)


def setup_inputs(seed: int = 0) -> dict:
    splits = jax.random.split(jax.random.key(seed), 12)
    return {
        "source_embedding_table": gaussian(splits[0], (N_SRC, N_DST, ROWS, D), 0.3, 1.75, ((0, 16), (1, 32)), jnp.float32),
        "source_adagrad_state": jnp.clip(jnp.exp(math.log(0.1) - 4.6051702 * jax.random.uniform(splits[1], (N_SRC, N_DST, ROWS), jnp.float32) ** steps_of(splits[1], (N_SRC, N_DST, ROWS), ((0, 16), (1, 32)), -0.2, 0.2)), 0.001, 0.1),
        "destination_embedding_table": gaussian(splits[2], (N_SRC, N_DST, ROWS, D), 0.3, 1.75, ((0, 16), (1, 32)), jnp.float32),
        "destination_adagrad_state": jnp.clip(jnp.exp(math.log(0.1) - 4.6051702 * jax.random.uniform(splits[3], (N_SRC, N_DST, ROWS), jnp.float32) ** steps_of(splits[3], (N_SRC, N_DST, ROWS), ((0, 16), (1, 32)), -0.2, 0.2)), 0.001, 0.1),
        "relations": gaussian(splits[4], (NREL, D), 1.0, 6.0, (), jnp.float32),
        "rel_state": jnp.clip(jnp.exp(math.log(0.1) - 4.6051702 * jax.random.uniform(splits[5], (NREL,), jnp.float32) ** steps_of(splits[5], (NREL,), ((0, 512),), -0.2, 0.2)), 0.001, 0.1),
        "source_edge_rows": plant(jax.random.randint(splits[6], (N_SRC, N_DST, STEPS, EDGES), 0, ROWS), jax.random.fold_in(splits[6], 1), 0, ROWS - 1).astype(jnp.int32),
        "destination_edge_rows": plant(jax.random.randint(splits[7], (N_SRC, N_DST, STEPS, EDGES), 0, ROWS), jax.random.fold_in(splits[7], 1), 0, ROWS - 1).astype(jnp.int32),
        "edge_relation_index": plant(jax.random.randint(splits[8], (N_SRC, N_DST, STEPS, EDGES), 0, NREL), jax.random.fold_in(splits[8], 1), 0, NREL - 1).astype(jnp.int32),
        "negative_block_rows": plant(jax.random.randint(splits[9], (N_SRC, N_DST, STEPS, GROUPS, NEG), 0, ROWS), jax.random.fold_in(splits[9], 1), 0, ROWS - 1).astype(jnp.int32),
        "bucket_block_counts": draw_bucket_block_counts(jax.random.fold_in(splits[11], 71), 0),
    }


def adagrad_update(block, state, grad):
    new_state = state + lax.optimization_barrier(jnp.mean(grad * grad, axis=-1))
    return (block - 0.1 * grad / jnp.sqrt(new_state)[:, None], new_state)

def group_terms(c, carry, src_blk, dst_blk, relations, s_rows, d_rows, r_ids, negs):
    grad_src, grad_dst, grad_rel = carry
    start = c * 128
    s_idx = lax.dynamic_slice_in_dim(s_rows, start, 128)
    d_idx = lax.dynamic_slice_in_dim(d_rows, start, 128)
    r_idx = lax.dynamic_slice_in_dim(r_ids, start, 128)
    n_idx = lax.dynamic_index_in_dim(negs, c, 0, keepdims=False)
    src_vec = src_blk[s_idx]
    dst_vec = dst_blk[d_idx]
    rel_vec = relations[r_idx]
    product = src_vec * rel_vec
    prod_low = product.astype(jnp.bfloat16)
    neg_low = dst_blk[n_idx].astype(jnp.bfloat16)
    positive = lax.optimization_barrier(jnp.sum(product * dst_vec, axis=-1))
    scores = lax.dot_general(prod_low, neg_low, (((1,), (1,)), ((), ())), preferred_element_type=jnp.float32)
    grad_pos = -jax.nn.sigmoid(-positive)
    grad_neg = (jax.nn.sigmoid(scores) / neg_low.shape[0]).astype(jnp.bfloat16)
    grad_prod = grad_pos[:, None] * dst_vec + jnp.dot(grad_neg, neg_low, preferred_element_type=jnp.float32)
    grad_negrows = lax.dot_general(grad_neg, prod_low, (((0,), (0,)), ((), ())), preferred_element_type=jnp.float32)
    grad_src = grad_src.at[s_idx].add(grad_prod * rel_vec)
    grad_dst = grad_dst.at[d_idx].add(grad_pos[:, None] * product).at[n_idx].add(grad_negrows)
    grad_rel = grad_rel.at[r_idx].add(grad_prod * src_vec)
    return (grad_src, grad_dst, grad_rel)

def reference(source_embedding_table, source_adagrad_state, destination_embedding_table, destination_adagrad_state, relations, rel_state, source_edge_rows, destination_edge_rows, edge_relation_index, negative_block_rows, bucket_block_counts):
    source_count, destination_count, gathered_rows, embedding_width = source_embedding_table.shape
    grad_rel = jnp.zeros(relations.shape, jnp.float32)
    present_source, present_source_state, present_destination, present_destination_state = (source_embedding_table, source_adagrad_state, destination_embedding_table, destination_adagrad_state)
    for iteration_index in range(STEPS):
        flattened_values = (present_source.reshape(-1, gathered_rows, embedding_width), present_source_state.reshape(-1, gathered_rows), present_destination.reshape(-1, gathered_rows, embedding_width), present_destination_state.reshape(-1, gathered_rows), source_edge_rows[:, :, iteration_index].reshape(-1, source_edge_rows.shape[-1]), destination_edge_rows[:, :, iteration_index].reshape(-1, source_edge_rows.shape[-1]), edge_relation_index[:, :, iteration_index].reshape(-1, source_edge_rows.shape[-1]), negative_block_rows[:, :, iteration_index].reshape(-1, negative_block_rows.shape[-2], negative_block_rows.shape[-1]), bucket_block_counts[:, :, iteration_index].reshape(-1))

        def one_bucket(relation_gradient, item):
            source_block_index, source_block_state, d_blk, d_st, s_r, d_r, r_i, negs, count = item
            zeros = jnp.zeros((gathered_rows, embedding_width), jnp.float32)

            def turn(c, carry):
                return group_terms(c, carry, source_block_index, d_blk, relations, s_r, d_r, r_i, negs)
            source_gradient, g_dst, relation_gradient = lax.fori_loop(jnp.int32(0), count.astype(jnp.int32), turn, (zeros, zeros, relation_gradient))
            updated_source_index, updated_source_state = adagrad_update(source_block_index, source_block_state, source_gradient)
            updated_destination_index, updated_destination = adagrad_update(d_blk, d_st, g_dst)
            return (relation_gradient, (updated_source_index, updated_source_state, updated_destination_index, updated_destination))
        grad_rel, loop_outputs = lax.scan(one_bucket, grad_rel, flattened_values)
        present_source = jnp.roll(loop_outputs[0].reshape(source_count, destination_count, gathered_rows, embedding_width), 1, axis=0)
        present_source_state = jnp.roll(loop_outputs[1].reshape(source_count, destination_count, gathered_rows), 1, axis=0)
        present_destination = jnp.roll(loop_outputs[2].reshape(source_count, destination_count, gathered_rows, embedding_width), 1, axis=1)
        present_destination_state = jnp.roll(loop_outputs[3].reshape(source_count, destination_count, gathered_rows), 1, axis=1)
    updated_relation, updated_relation_state = adagrad_update(relations, rel_state, grad_rel)
    return (present_source, present_source_state, present_destination, present_destination_state, updated_relation, updated_relation_state)
```

```python
import jax
import jax.numpy as jnp
from jax import lax
from jax.experimental import pallas as pl
from jax.experimental.pallas import tpu as pltpu
from jax.sharding import PartitionSpec as P

MESH = pl.DeviceIdType.MESH
ORDERS = (("z", "y", "x"), ("y", "x", "z"), ("x", "z", "y"))
SIZE = {"x": 4, "y": 8, "z": 8}
ROUND = ((2, 0), (0, 0), (1, 0), (2, 1), (0, 1), (1, 1), (2, 2), (0, 2), (1, 2))


def shifted(block, axis, distance):
    devices = range(lax.axis_size(axis))
    route = [((i - distance) % len(devices), i) for i in devices]
    return lax.ppermute(block, axis, route)


def adagrad_update(block, state, grad):
    new_state = state + jnp.mean(grad * grad, axis=-1)
    return (block - 0.1 * grad / jnp.sqrt(new_state)[:, None], new_state)


def group_terms(c, carry, src_blk, dst_blk, relations, s_rows, d_rows, r_ids, negs):
    grad_src, grad_dst, grad_rel = carry
    start = c * 128
    s_idx = lax.dynamic_slice_in_dim(s_rows, start, 128)
    d_idx = lax.dynamic_slice_in_dim(d_rows, start, 128)
    r_idx = lax.dynamic_slice_in_dim(r_ids, start, 128)
    n_idx = lax.dynamic_index_in_dim(negs, c, 0, keepdims=False)
    src_vec = src_blk[s_idx]
    dst_vec = dst_blk[d_idx]
    rel_vec = relations[r_idx]
    product = src_vec * rel_vec
    prod_low = product.astype(jnp.bfloat16)
    neg_low = dst_blk[n_idx].astype(jnp.bfloat16)
    positive = jnp.sum(product * dst_vec, axis=-1)
    scores = lax.dot_general(
        prod_low, neg_low, (((1,), (1,)), ((), ())), preferred_element_type=jnp.float32
    )
    grad_pos = -jax.nn.sigmoid(-positive)
    grad_neg = (jax.nn.sigmoid(scores) / neg_low.shape[0]).astype(jnp.bfloat16)
    grad_prod = grad_pos[:, None] * dst_vec + jnp.dot(
        grad_neg, neg_low, preferred_element_type=jnp.float32
    )
    grad_negrows = lax.dot_general(
        grad_neg, prod_low, (((0,), (0,)), ((), ())), preferred_element_type=jnp.float32
    )
    grad_src = grad_src.at[s_idx].add(grad_prod * rel_vec)
    grad_dst = grad_dst.at[d_idx].add(grad_pos[:, None] * product).at[n_idx].add(grad_negrows)
    grad_rel = grad_rel.at[r_idx].add(grad_prod * src_vec)
    return (grad_src, grad_dst, grad_rel)


def coords():
    s, d = lax.axis_index("src"), lax.axis_index("dst")
    return {
        "core": lax.rem(s, 2),
        "x": lax.rem(lax.div(s, 2), 4),
        "y": lax.div(s, 8) * 4 + lax.rem(d, 4),
        "z": lax.div(d, 4),
    }


def device_of(at):
    return (
        lax.div(at["y"], 4) * 8 + at["x"] * 2 + at["core"],
        at["z"] * 4 + lax.rem(at["y"], 4),
    )


def partner(me, axis, offset):
    return device_of({**me, axis: lax.rem(me[axis] + offset, SIZE[axis])})


def sum_kernel(g_ref, out_ref, core_in, *rest):
    half = rest[0]
    recv = {(c, p): rest[1 + c * 3 + p] for c in range(3) for p in range(3)}
    held = {(c, p): rest[10 + c * 2 + p] for c in range(3) for p in range(2)}
    core_sem, send_sem, recv_sem = rest[16:]
    me = coords()
    sibling = device_of({**me, "core": 1 - me["core"]})
    barrier = pltpu.get_barrier_semaphore()
    pl.semaphore_signal(barrier, inc=1, device_id=sibling, device_id_type=MESH)
    for axis in "xyz":

        @pl.loop(1, SIZE[axis])
        def _(o):
            pl.semaphore_signal(
                barrier, inc=1, device_id=partner(me, axis, o), device_id_type=MESH
            )

    pl.semaphore_wait(barrier, 18)

    def core_copy(c):
        return pltpu.make_async_remote_copy(
            g_ref.at[c, 1 - me["core"]],
            core_in.at[c],
            core_sem.at[0, c],
            core_sem.at[1, c],
            device_id=sibling,
            device_id_type=MESH,
        )

    def rows_of(c, p, j):
        if p == 2:
            return pl.ds(pl.multiple_of(lax.div(j, 2) * 8, 8), 8)
        count = recv[c, p].shape[1]
        return pl.ds(pl.multiple_of(j * count, count), count)

    def start_phase(c, p):
        axis = ORDERS[c][p]
        source = half.at[c] if p == 0 else held[c, p - 1]

        @pl.loop(1, SIZE[axis])
        def _(o):
            target = lax.rem(me[axis] + o, SIZE[axis])
            pltpu.make_async_remote_copy(
                source.at[rows_of(c, p, target)],
                recv[c, p].at[o - 1],
                send_sem.at[c, p],
                recv_sem.at[c, p],
                device_id=partner(me, axis, o),
                device_id_type=MESH,
            ).start()

    def finish_phase(c, p):
        axis = ORDERS[c][p]
        pltpu.make_async_remote_copy(
            recv[c, p],
            recv[c, p],
            send_sem.at[c, p],
            recv_sem.at[c, p],
            device_id=sibling,
            device_id_type=MESH,
        ).wait()
        source = half.at[c] if p == 0 else held[c, p - 1]
        total = source[rows_of(c, p, me[axis]), :]
        for o in range(SIZE[axis] - 1):
            total = total + recv[c, p][o]
        return total

    for c in (2, 0, 1):
        core_copy(c).start()
    for c in (2, 0, 1):
        core_copy(c).wait()
        half[c] = g_ref[c, me["core"]] + core_in[c]
        start_phase(c, 0)
    for c, p in ROUND:
        total = finish_phase(c, p)
        if p < 2:
            held[c, p][...] = total
            start_phase(c, p + 1)
        else:
            odd = lax.rem(me[ORDERS[c][2]], 2)
            out_ref[:, c * 128 : (c + 1) * 128] = jnp.where(odd == 0, total[0:4], total[4:8])


def relation_total(grad_rel):
    g = grad_rel.reshape(2, 4, 2, 8, 4, 4, 3, 128)
    thirds = (
        g[..., 0, :].transpose(2, 3, 0, 4, 1, 5, 6),
        g[..., 1, :].transpose(2, 0, 4, 1, 3, 5, 6),
        g[..., 2, :].transpose(2, 1, 3, 0, 4, 5, 6),
    )
    g = jnp.stack([t.reshape(2, 1024, 128) for t in thirds])
    chunk = ((128, 16, 8), (128, 32, 8), (256, 32, 8))
    scratch = [pltpu.VMEM((3, 1024, 128), jnp.float32), pltpu.VMEM((3, 1024, 128), jnp.float32)]
    for c in range(3):
        for p in range(3):
            scratch.append(pltpu.VMEM((SIZE[ORDERS[c][p]] - 1, chunk[c][p], 128), jnp.float32))
    for c in range(3):
        for p in range(2):
            scratch.append(pltpu.VMEM((chunk[c][p], 128), jnp.float32))
    scratch += [
        pltpu.SemaphoreType.DMA((2, 3)),
        pltpu.SemaphoreType.DMA((3, 3)),
        pltpu.SemaphoreType.DMA((3, 3)),
    ]
    return pl.pallas_call(
        sum_kernel,
        out_shape=jax.ShapeDtypeStruct((4, 384), jnp.float32),
        in_specs=[pl.BlockSpec(memory_space=pltpu.VMEM)],
        out_specs=pl.BlockSpec(memory_space=pltpu.VMEM),
        scratch_shapes=scratch,
        compiler_params=pltpu.CompilerParams(
            collective_id=0, has_side_effects=True, vmem_limit_bytes=32 * 2**20
        ),
    )(g)


def on_device(
    source_embedding_table,
    source_adagrad_state,
    destination_embedding_table,
    destination_adagrad_state,
    relations,
    rel_state,
    source_edge_rows,
    destination_edge_rows,
    edge_relation_index,
    negative_block_rows,
    bucket_block_counts,
):
    src_blk, src_st = (source_embedding_table[0, 0], source_adagrad_state[0, 0])
    dst_blk, dst_st = (destination_embedding_table[0, 0], destination_adagrad_state[0, 0])
    grad_rel = jnp.zeros(relations.shape, jnp.float32)
    zeros = jnp.zeros(src_blk.shape, jnp.float32)
    for iteration_index in range(source_edge_rows.shape[2]):
        s_rows = source_edge_rows[0, 0, iteration_index]
        d_rows = destination_edge_rows[0, 0, iteration_index]
        r_ids = edge_relation_index[0, 0, iteration_index]
        negs = negative_block_rows[0, 0, iteration_index]
        live = bucket_block_counts[0, 0, iteration_index]
        s_cur, d_cur = (src_blk, dst_blk)

        def turn(c, carry):
            return group_terms(c, carry, s_cur, d_cur, relations, s_rows, d_rows, r_ids, negs)

        grad_src, grad_dst, grad_rel = lax.fori_loop(
            jnp.int32(0), live, turn, (zeros, zeros, grad_rel)
        )
        src_blk, src_st = adagrad_update(src_blk, src_st, grad_src)
        dst_blk, dst_st = adagrad_update(dst_blk, dst_st, grad_dst)
        src_blk, src_st = shifted((src_blk, src_st), "src", 1)
        dst_blk, dst_st = shifted((dst_blk, dst_st), "dst", 1)
    share = rel_state.shape[0]
    first = lax.axis_index(("src", "dst")) * share
    own_grad = relation_total(grad_rel)
    own_rel = lax.dynamic_slice_in_dim(relations, first, share, 0)
    updated_relation, updated_relation_state = adagrad_update(own_rel, rel_state, own_grad)
    return (
        src_blk[None, None],
        src_st[None, None],
        dst_blk[None, None],
        dst_st[None, None],
        updated_relation,
        updated_relation_state,
    )


def solution(mesh):
    in_specs = (
        P("src", "dst", None, None),
        P("src", "dst", None),
        P("src", "dst", None, None),
        P("src", "dst", None),
        P(),
        P(("src", "dst")),
        P("src", "dst", None, None),
        P("src", "dst", None, None),
        P("src", "dst", None, None),
        P("src", "dst", None, None, None),
        P("src", "dst", None),
    )
    out_specs = (
        P("src", "dst", None, None),
        P("src", "dst", None),
        P("src", "dst", None, None),
        P("src", "dst", None),
        P(("src", "dst"), None),
        P(("src", "dst")),
    )
    return jax.shard_map(
        on_device, mesh=mesh, in_specs=in_specs, out_specs=out_specs, check_vma=False
    )
```

```python
import jax
import jax.numpy as jnp
from jax import lax
from jax.experimental import pallas as pl
from jax.experimental.pallas import tpu as pltpu
from jax.sharding import PartitionSpec as P

MESH = pl.DeviceIdType.MESH
F32, BF16, I32 = jnp.float32, jnp.bfloat16, jnp.int32
ORDERS = (("z", "y", "x"), ("y", "x", "z"), ("x", "z", "y"))
CHUNK = ((128, 16, 8), (128, 32, 8), (256, 32, 8))
SIZE = {"x": 4, "y": 8, "z": 8}
ROUND = ((2, 0), (0, 0), (1, 0), (2, 1), (0, 1), (1, 1), (2, 2), (0, 2), (1, 2))
STEPS = 3
EDGES_1, EDGES_2, NEXT, SRC_END, DST_END = (0, 31), (0, 30), (1, 31), (1, 2), (0, 3)


def coords():
    s, d = lax.axis_index("src"), lax.axis_index("dst")
    return {
        "core": lax.rem(s, 2),
        "x": lax.rem(lax.div(s, 2), 4),
        "y": lax.div(s, 8) * 4 + lax.rem(d, 4),
        "z": lax.div(d, 4),
    }


def device_of(at):
    return (
        lax.div(at["y"], 4) * 8 + at["x"] * 2 + at["core"],
        at["z"] * 4 + lax.rem(at["y"], 4),
    )


def partner(me, axis, offset):
    return device_of({**me, axis: lax.rem(me[axis] + offset, SIZE[axis])})


def moved(offset):
    s, d = lax.axis_index("src"), lax.axis_index("dst")
    return (lax.rem(s + offset[0], 16), lax.rem(d + offset[1], 32))


def dot(a, b):
    return jnp.dot(a, b, preferred_element_type=F32)


def dot_nt(a, b):
    return lax.dot_general(a, b, (((1,), (1,)), ((), ())), preferred_element_type=F32)


def one_hot(mask):
    return jnp.where(mask, 1.0, 0.0).astype(BF16)


def split(value, axis=0):
    high = value.astype(BF16)
    low = (value - high.astype(F32)).astype(BF16)
    return jnp.concatenate([high, low], axis=axis)


def sigmoid(value):
    return 1.0 / (1.0 + jnp.exp(-value))


def eye():
    return lax.broadcasted_iota(I32, (128, 128), 0) == lax.broadcasted_iota(I32, (128, 128), 1)


def as_column(row):
    return jnp.sum(jnp.where(eye(), row, 0.0), axis=1, keepdims=True)


def as_row(column):
    return jnp.sum(jnp.where(eye(), column, 0.0), axis=0, keepdims=True)


def adagrad(block, state_row, grad):
    state = as_column(state_row) + jnp.sum(grad * grad, axis=1, keepdims=True) * (1.0 / 384)
    return block - 0.1 * grad / jnp.sqrt(state), as_row(state)


def positions(r, c):
    k, z, x = r & 3, (r >> 4) & 7, (r >> 8) & 3
    y = ((r >> 10) << 2) | ((r >> 2) & 3)
    if c == 0:
        return (((z * 8 + y) * 4 + x) * 4) + k
    if c == 1:
        return (((y * 4 + x) * 8 + z) * 4) + k
    return (((x * 8 + z) * 8 + y) * 4) + k


def window_kernel(
    src_ref, src_st_ref, dst_ref, dst_st_ref, rel_hbm, rel_st_ref, idx_ref,
    src_out, src_st_out, dst_out, dst_st_out, rel_out, rel_st_out,
    table, idx, idx_sib, idx_smem, src_in, src_st_in, src_new, src_st_new, dst_cur, dst_st_cur,
    rel_vec, v_own, v_sib, half, *rest,
):
    recv = {(c, p): rest[c * 3 + p] for c in range(3) for p in range(3)}
    held = {(c, p): rest[9 + c * 2 + p] for c in range(3) for p in range(2)}
    (table_sem, smem_sem, idx_sem, sib_idx_sem, block_sem, state_sem, v_sem, end_sem,
     send_sem, recv_sem) = rest[15:]
    me = coords()
    sibling = device_of({**me, "core": 1 - me["core"]})

    load_table = pltpu.make_async_copy(rel_hbm, table, table_sem)
    load_table.start()

    barrier = pltpu.get_barrier_semaphore()
    pl.semaphore_signal(barrier, inc=1, device_id=sibling, device_id_type=MESH)
    for axis in "xyz":

        @pl.loop(1, SIZE[axis])
        def _(o):
            pl.semaphore_signal(
                barrier, inc=1, device_id=partner(me, axis, o), device_id_type=MESH
            )

    for ds, dd in (EDGES_1, EDGES_2, NEXT, SRC_END, DST_END):
        for offset in ((ds, dd), ((16 - ds) % 16, (32 - dd) % 32)):
            pl.semaphore_signal(barrier, inc=1, device_id=moved(offset), device_id_type=MESH)

    idx[0] = idx_ref[0]
    src_in[0] = src_ref[...]
    src_st_in[0] = src_st_ref[...]
    dst_cur[...] = dst_ref[...]
    dst_st_cur[...] = dst_st_ref[...]
    half[...] = jnp.zeros_like(half)
    pl.semaphore_wait(barrier, 28)

    def remote(source, target, sems, to):
        return pltpu.make_async_remote_copy(
            source, target, sems.at[0], sems.at[1], device_id=to, device_id_type=MESH
        )

    def edge_copy(t, offset):
        return remote(idx_ref.at[t], idx.at[t], idx_sem.at[t], moved(offset))

    def sib_idx_copy(t):
        return remote(idx.at[t], idx_sib.at[t], sib_idx_sem.at[t], sibling)

    def v_copy(t):
        return remote(v_own.at[t], v_sib.at[t], v_sem.at[t], sibling)

    def block_copy(t):
        return remote(src_new.at[t], src_in.at[t + 1], block_sem.at[t], moved(NEXT))

    def state_copy(t):
        return remote(src_st_new.at[t], src_st_in.at[t + 1], state_sem.at[t], moved(NEXT))

    edges = (None, edge_copy(1, EDGES_1), edge_copy(2, EDGES_2))
    edges[1].start()
    edges[2].start()
    sib_idx_copy(0).start()

    def gather_relations(t):
        load = pltpu.make_async_copy(idx.at[t], idx_smem.at[t], smem_sem)
        load.start()
        load.wait()

        @pl.loop(0, 32)
        def _(i):
            for j in range(8):
                e = i * 8 + j
                rel_vec[pl.ds(e, 1), :] = table[pl.ds(idx_smem[t, 2, e], 1), :]

    def add_third(t, c):
        v = jnp.concatenate(
            [v_own[t, :, c * 128 : (c + 1) * 128], v_sib[t, :, c * 128 : (c + 1) * 128]], axis=0
        )
        rhs = split(v, axis=1)
        r = jnp.concatenate([idx[t, 2:3, :], idx_sib[t, 2:3, :]], axis=1)
        at = jnp.where(((r >> 7) & 1) == me["core"], positions(r, c), -1)

        @pl.loop(0, 4)
        def _(ch):
            rows = pl.ds(pl.multiple_of(ch * 256, 256), 256)
            hot = one_hot(lax.broadcasted_iota(I32, (256, 512), 0) + ch * 256 == at)
            both = dot(hot, rhs)
            half[c, rows, :] += both[:, :128] + both[:, 128:]

    def work(t):
        rows = idx[t]
        columns = jnp.transpose(rows.astype(F32)).astype(I32)
        s_col, d_col, n_col = columns[:, 0:1], columns[:, 1:2], columns[:, 3:4]
        live = columns[:, 4:5].astype(F32)
        lanes = lax.broadcasted_iota(I32, (256, 256), 1) & 127
        src_blk, dst_blk = src_in[t], dst_cur[...]
        dst_two = split(dst_blk)
        src_vec = dot(one_hot(lanes == s_col), split(src_blk))
        dst_vec = dot(one_hot(lanes == d_col), dst_two)
        negb = dot(one_hot(lanes[:, :128] == n_col), dst_two[:128]).astype(BF16)
        rel = rel_vec[...]
        a = src_vec * rel
        ab = a.astype(BF16)
        pos = jnp.sum(a * dst_vec, axis=1, keepdims=True)
        gpos = -sigmoid(-pos) * live
        negs_part, rows_part = [], []
        for c in range(2):
            block = slice(c * 128, (c + 1) * 128)
            neg = dot_nt(ab[block], negb[block])
            gneg = sigmoid(neg) * (1.0 / 128) * live[block]
            negs_part.append(dot(gneg.astype(BF16), negb[block]))
            rows_part.append(dot(jnp.transpose(gneg).astype(BF16), ab[block]))
        gprod = gpos * dst_vec + jnp.concatenate(negs_part, axis=0)
        v_own[t] = gprod * src_vec
        v_copy(t).start()
        subl = lax.broadcasted_iota(I32, (128, 256), 0)
        s_hot = one_hot(subl == rows[0:1])
        grad_src = dot(jnp.concatenate([s_hot, s_hot], axis=1), split(gprod * rel))
        block, state = adagrad(src_blk, src_st_in[t], grad_src)
        src_new[t] = block
        src_st_new[t] = state

        @pl.when(t < 2)
        def _():
            state_copy(t).start()
            block_copy(t).start()

        d_hot = one_hot(subl == rows[1:2])
        n_hot = one_hot(subl == rows[3:4])
        grad_dst = dot(
            jnp.concatenate([d_hot, d_hot, n_hot, n_hot], axis=1),
            jnp.concatenate([split(gpos * a), split(jnp.concatenate(rows_part, axis=0))], axis=0),
        )
        block, state = adagrad(dst_blk, dst_st_cur[...], grad_dst)
        dst_cur[...] = block
        dst_st_cur[...] = state

    load_table.wait()

    @pl.loop(0, STEPS)
    def _(t):
        @pl.when(t > 0)
        def _():
            edge_copy(t, EDGES_1).wait()
            sib_idx_copy(t).start()

        gather_relations(t)

        @pl.when(t > 0)
        def _():
            sib_idx_copy(t - 1).wait()
            v_copy(t - 1).wait()
            for c in range(3):
                add_third(t - 1, c)
            state_copy(t - 1).wait()
            block_copy(t - 1).wait()

        work(t)

    ends = [
        remote(src_st_new.at[2], src_st_out, end_sem.at[0], moved(SRC_END)),
        remote(dst_st_cur, dst_st_out, end_sem.at[1], moved(DST_END)),
        remote(src_new.at[2], src_out, end_sem.at[2], moved(SRC_END)),
        remote(dst_cur, dst_out, end_sem.at[3], moved(DST_END)),
    ]

    def rows_of(c, p, j):
        if p == 2:
            return pl.ds(pl.multiple_of(lax.div(j, 2) * 8, 8), 8)
        return pl.ds(pl.multiple_of(j * CHUNK[c][p], CHUNK[c][p]), CHUNK[c][p])

    def start_phase(c, p):
        axis = ORDERS[c][p]
        source = half.at[c] if p == 0 else held[c, p - 1]

        @pl.loop(1, SIZE[axis])
        def _(o):
            target = lax.rem(me[axis] + o, SIZE[axis])
            pltpu.make_async_remote_copy(
                source.at[rows_of(c, p, target)],
                recv[c, p].at[o - 1],
                send_sem.at[c, p],
                recv_sem.at[c, p],
                device_id=partner(me, axis, o),
                device_id_type=MESH,
            ).start()

    def finish_phase(c, p):
        axis = ORDERS[c][p]
        pltpu.make_async_remote_copy(
            recv[c, p],
            recv[c, p],
            send_sem.at[c, p],
            recv_sem.at[c, p],
            device_id=sibling,
            device_id_type=MESH,
        ).wait()
        source = half.at[c] if p == 0 else held[c, p - 1]
        total = source[rows_of(c, p, me[axis]), :]
        for o in range(SIZE[axis] - 1):
            total = total + recv[c, p][o]
        return total

    sib_idx_copy(2).wait()
    v_copy(2).wait()
    for c in (2, 0, 1):
        add_third(2, c)
        start_phase(c, 0)
    for copy in ends:
        copy.start()
    last = {}
    for c, p in ROUND:
        total = finish_phase(c, p)
        if p < 2:
            held[c, p][...] = total
            start_phase(c, p + 1)
        else:
            odd = lax.rem(me[ORDERS[c][2]], 2)
            last[c] = jnp.where(odd == 0, total[0:4], total[4:8])
    grad = jnp.concatenate([last[0], last[1], last[2]], axis=1)
    owner = lax.axis_index("src") * 32 + lax.axis_index("dst")
    near = table[pl.ds(pl.multiple_of(lax.div(owner, 2) * 8, 8), 8), :]
    own = jnp.where(lax.rem(owner, 2) == 0, near[0:4], near[4:8])
    state = rel_st_ref[...] + jnp.sum(grad * grad, axis=1, keepdims=True) * (1.0 / 384)
    rel_st_out[...] = state
    rel_out[...] = own - 0.1 * grad / jnp.sqrt(state)
    for copy in ends:
        copy.wait()


def on_device(
    source_embedding_table,
    source_adagrad_state,
    destination_embedding_table,
    destination_adagrad_state,
    relations,
    rel_state,
    source_edge_rows,
    destination_edge_rows,
    edge_relation_index,
    negative_block_rows,
    bucket_block_counts,
):
    counts = bucket_block_counts[0, 0]
    live = (jnp.arange(256, dtype=I32)[None, :] // 128 < counts[:, None]).astype(I32)
    idx = jnp.stack(
        [
            source_edge_rows[0, 0],
            destination_edge_rows[0, 0],
            edge_relation_index[0, 0],
            negative_block_rows[0, 0].reshape(STEPS, 256),
            live,
            live,
            live,
            live,
        ],
        axis=1,
    )
    vmem = pl.BlockSpec(memory_space=pltpu.VMEM)
    dma = pltpu.SemaphoreType.DMA
    scratch = [
        pltpu.VMEM((2048, 384), F32),
        pltpu.VMEM((3, 8, 256), I32),
        pltpu.VMEM((3, 8, 256), I32),
        pltpu.SMEM((3, 8, 256), I32),
        pltpu.VMEM((3, 128, 384), F32),
        pltpu.VMEM((3, 1, 128), F32),
        pltpu.VMEM((3, 128, 384), F32),
        pltpu.VMEM((3, 1, 128), F32),
        pltpu.VMEM((128, 384), F32),
        pltpu.VMEM((1, 128), F32),
        pltpu.VMEM((256, 384), F32),
        pltpu.VMEM((3, 256, 384), F32),
        pltpu.VMEM((3, 256, 384), F32),
        pltpu.VMEM((3, 1024, 128), F32),
    ]
    for c in range(3):
        for p in range(3):
            scratch.append(pltpu.VMEM((SIZE[ORDERS[c][p]] - 1, CHUNK[c][p], 128), F32))
    for c in range(3):
        for p in range(2):
            scratch.append(pltpu.VMEM((CHUNK[c][p], 128), F32))
    scratch += [dma, dma, dma((3, 2)), dma((3, 2)), dma((2, 2)), dma((2, 2)), dma((3, 2)), dma((4, 2))]
    scratch += [dma((3, 3)), dma((3, 3))]
    block = jax.ShapeDtypeStruct((128, 384), F32)
    row = jax.ShapeDtypeStruct((1, 128), F32)
    src_out, src_st, dst_out, dst_st, rel_out, rel_st = pl.pallas_call(
        window_kernel,
        out_shape=(
            block,
            row,
            block,
            row,
            jax.ShapeDtypeStruct((4, 384), F32),
            jax.ShapeDtypeStruct((4, 1), F32),
        ),
        in_specs=[vmem, vmem, vmem, vmem, pl.BlockSpec(memory_space=pl.ANY), vmem, vmem],
        out_specs=(vmem,) * 6,
        scratch_shapes=scratch,
        compiler_params=pltpu.CompilerParams(
            collective_id=0, has_side_effects=True, vmem_limit_bytes=40 * 2**20
        ),
    )(
        source_embedding_table[0, 0],
        source_adagrad_state[0],
        destination_embedding_table[0, 0],
        destination_adagrad_state[0],
        relations,
        rel_state[:, None],
        idx,
    )
    return (
        src_out[None, None],
        src_st[None],
        dst_out[None, None],
        dst_st[None],
        rel_out,
        rel_st[:, 0],
    )


def solution(mesh):
    in_specs = (
        P("src", "dst", None, None),
        P("src", "dst", None),
        P("src", "dst", None, None),
        P("src", "dst", None),
        P(),
        P(("src", "dst")),
        P("src", "dst", None, None),
        P("src", "dst", None, None),
        P("src", "dst", None, None),
        P("src", "dst", None, None, None),
        P("src", "dst", None),
    )
    out_specs = (
        P("src", "dst", None, None),
        P("src", "dst", None),
        P("src", "dst", None, None),
        P("src", "dst", None),
        P(("src", "dst"), None),
        P(("src", "dst")),
    )
    return jax.shard_map(
        on_device, mesh=mesh, in_specs=in_specs, out_specs=out_specs, check_vma=False
    )
```

```python
import jax
import jax.numpy as jnp
from jax import lax
from jax.experimental import pallas as pl
from jax.experimental.pallas import tpu as pltpu
from jax.sharding import PartitionSpec as P

MESH = pl.DeviceIdType.MESH
F32, BF16, I32 = jnp.float32, jnp.bfloat16, jnp.int32
ORDERS = (("z", "y", "x"), ("y", "x", "z"), ("x", "z", "y"))
CHUNK = ((128, 16, 8), (128, 32, 8), (256, 32, 8))
SIZE = {"x": 4, "y": 8, "z": 8}
ROUND = ((2, 0), (0, 0), (1, 0), (2, 1), (0, 1), (1, 1), (2, 2), (0, 2), (1, 2))
STEPS = 3
VMEM_LIMIT = 60 * 2**20
EDGES_1, EDGES_2, NEXT, SRC_END, DST_END = (0, 31), (0, 30), (1, 31), (1, 2), (0, 3)


def coords():
    s, d = lax.axis_index("src"), lax.axis_index("dst")
    return {
        "core": lax.rem(s, 2),
        "x": lax.rem(lax.div(s, 2), 4),
        "y": lax.div(s, 8) * 4 + lax.rem(d, 4),
        "z": lax.div(d, 4),
    }


def device_of(at):
    return (
        lax.div(at["y"], 4) * 8 + at["x"] * 2 + at["core"],
        at["z"] * 4 + lax.rem(at["y"], 4),
    )


def partner(me, axis, offset):
    return device_of({**me, axis: lax.rem(me[axis] + offset, SIZE[axis])})


def moved(offset):
    s, d = lax.axis_index("src"), lax.axis_index("dst")
    return (lax.rem(s + offset[0], 16), lax.rem(d + offset[1], 32))


def dot(a, b):
    return jnp.dot(a, b, preferred_element_type=F32)


def dot_nt(a, b):
    return lax.dot_general(a, b, (((1,), (1,)), ((), ())), preferred_element_type=F32)


def one_hot(mask):
    return jnp.where(mask, 1.0, 0.0).astype(BF16)


def split(value, axis=0):
    high = value.astype(BF16)
    low = (value - high.astype(F32)).astype(BF16)
    return jnp.concatenate([high, low], axis=axis)


def sigmoid(value):
    return 1.0 / (1.0 + jnp.exp(-value))


def eye(n):
    return lax.broadcasted_iota(I32, (n, n), 0) == lax.broadcasted_iota(I32, (n, n), 1)


def as_column(row):
    return jnp.sum(jnp.where(eye(row.shape[1]), row, 0.0), axis=1, keepdims=True)


def as_row(column):
    return jnp.sum(jnp.where(eye(column.shape[0]), column, 0.0), axis=0, keepdims=True)


def adagrad(block, state_row, grad):
    state = as_column(state_row) + jnp.sum(grad * grad, axis=1, keepdims=True) * (1.0 / 384)
    return block - 0.1 * grad / jnp.sqrt(state), as_row(state)


def positions(r, c):
    k, z, x = r & 3, (r >> 4) & 7, (r >> 8) & 3
    y = ((r >> 10) << 2) | ((r >> 2) & 3)
    if c == 0:
        return (((z * 8 + y) * 4 + x) * 4) + k
    if c == 1:
        return (((y * 4 + x) * 8 + z) * 4) + k
    return (((x * 8 + z) * 8 + y) * 4) + k


def window_kernel(
    src_hbm, src_st_hbm, dst_hbm, dst_st_hbm, rel_hbm, rel_st_hbm, s_hbm, d_hbm, r_hbm, n_hbm, count_hbm,
    src_out, src_st_out, dst_out, dst_st_out, rel_out, rel_st_out,
    table, rel_st, s_raw, d_raw, r_raw, n_raw, r_smem, count_smem,
    idx_mine, idx, idx_sib, idx_smem, src_in, src_st_in, src_new, src_st_new, dst_cur, dst_st_cur,
    rel_vec, v_own, v_sib, half, *rest,
):
    recv = {(c, p): rest[c * 3 + p] for c in range(3) for p in range(3)}
    held = {(c, p): rest[9 + c * 2 + p] for c in range(3) for p in range(2)}
    (load_sem, smem_sem, idx_sem, sib_idx_sem, block_sem, state_sem, v_sem, end_sem,
     send_sem, recv_sem) = rest[15:]
    me = coords()
    sibling = device_of({**me, "core": 1 - me["core"]})

    loads = [
        pltpu.make_async_copy(source, target, load_sem.at[i])
        for i, (source, target) in enumerate(
            [
                (r_hbm, r_smem), (count_hbm, count_smem), (rel_hbm, table),
                (s_hbm, s_raw), (d_hbm, d_raw), (r_hbm, r_raw), (n_hbm, n_raw),
                (src_hbm, src_in.at[0]), (dst_hbm, dst_cur),
                (src_st_hbm, src_st_in.at[0]), (dst_st_hbm, dst_st_cur), (rel_st_hbm, rel_st),
            ]
        )
    ]
    for load in loads:
        load.start()

    barrier = pltpu.get_barrier_semaphore()
    pl.semaphore_signal(barrier, inc=1, device_id=sibling, device_id_type=MESH)
    for ds, dd in (NEXT, EDGES_1, EDGES_2, SRC_END, DST_END):
        for offset in ((ds, dd), ((16 - ds) % 16, (32 - dd) % 32)):
            pl.semaphore_signal(barrier, inc=1, device_id=moved(offset), device_id_type=MESH)

    for axis in "xyz":

        @pl.loop(1, SIZE[axis])
        def _(o):
            pl.semaphore_signal(
                barrier, inc=1, device_id=partner(me, axis, o), device_id_type=MESH
            )

    half[...] = jnp.zeros_like(half)
    for load in loads:
        load.wait()
    block_of = lax.broadcasted_iota(I32, (1, 256), 1) >> 7
    for t in range(STEPS):
        idx_mine[t, 0:1, :] = s_raw[t]
        idx_mine[t, 1:2, :] = d_raw[t]
        idx_mine[t, 2:3, :] = r_raw[t]
        idx_mine[t, 3:4, 0:128] = n_raw[t, 0:1, :]
        idx_mine[t, 3:4, 128:256] = n_raw[t, 1:2, :]
        live = jnp.where(block_of < count_smem[0, t], 1, 0)
        idx_mine[t, 4:8, :] = jnp.broadcast_to(live, (4, 256))
    idx[0] = idx_mine[0]

    def remote(source, target, sems, to):
        return pltpu.make_async_remote_copy(
            source, target, sems.at[0], sems.at[1], device_id=to, device_id_type=MESH
        )

    def edge_copy(t, offset):
        return remote(idx_mine.at[t], idx.at[t], idx_sem.at[t], moved(offset))

    def sib_idx_copy(t):
        return remote(idx.at[t], idx_sib.at[t], sib_idx_sem.at[t], sibling)

    def v_copy(t):
        return remote(v_own.at[t], v_sib.at[t], v_sem.at[t], sibling)

    def block_copy(t):
        return remote(src_new.at[t], src_in.at[t + 1], block_sem.at[t], moved(NEXT))

    def state_copy(t):
        return remote(src_st_new.at[t], src_st_in.at[t + 1], state_sem.at[t], moved(NEXT))

    ends = [
        remote(src_st_new.at[2], src_st_out, end_sem.at[0], moved(SRC_END)),
        remote(src_new.at[2], src_out, end_sem.at[1], moved(SRC_END)),
        remote(dst_st_cur, dst_st_out, end_sem.at[2], moved(DST_END)),
        remote(dst_cur, dst_out, end_sem.at[3], moved(DST_END)),
    ]

    def gather_relations(row_of):
        @pl.loop(0, 32)
        def _(i):
            for j in range(8):
                e = i * 8 + j
                rel_vec[pl.ds(e, 1), :] = table[pl.ds(row_of(e), 1), :]

    def add_third(t, c):
        v = jnp.concatenate(
            [v_own[t, :, c * 128 : (c + 1) * 128], v_sib[t, :, c * 128 : (c + 1) * 128]], axis=0
        )
        rhs = split(v, axis=1)
        r = jnp.concatenate([idx[t, 2:3, :], idx_sib[t, 2:3, :]], axis=1)
        at = jnp.where(((r >> 7) & 1) == me["core"], positions(r, c), -1)

        @pl.loop(0, 4)
        def _(ch):
            rows = pl.ds(pl.multiple_of(ch * 256, 256), 256)
            hot = one_hot(lax.broadcasted_iota(I32, (256, 512), 0) + ch * 256 == at)
            both = dot(hot, rhs)
            half[c, rows, :] += both[:, :128] + both[:, 128:]

    def work(t, send_v, send_src):
        rows = idx[t]
        columns = jnp.transpose(rows.astype(F32)).astype(I32)
        s_col, d_col, n_col = columns[:, 0:1], columns[:, 1:2], columns[:, 3:4]
        live = columns[:, 4:5].astype(F32)
        lanes = lax.broadcasted_iota(I32, (256, 256), 1) & 127
        src_blk, dst_blk = src_in[t], dst_cur[...]
        dst_two = split(dst_blk)
        src_vec = dot(one_hot(lanes == s_col), split(src_blk))
        dst_vec = dot(one_hot(lanes == d_col), dst_two)
        negb = dot(one_hot(lanes[:, :128] == n_col), dst_two[:128]).astype(BF16)
        rel = rel_vec[...]
        a = src_vec * rel
        ab = a.astype(BF16)
        pos = jnp.sum(a * dst_vec, axis=1, keepdims=True)
        gpos = -sigmoid(-pos) * live
        negs_part, rows_part = [], []
        for c in range(2):
            block = slice(c * 128, (c + 1) * 128)
            neg = dot_nt(ab[block], negb[block])
            gneg = sigmoid(neg) * (1.0 / 128) * live[block]
            negs_part.append(dot(gneg.astype(BF16), negb[block]))
            rows_part.append(dot(jnp.transpose(gneg).astype(BF16), ab[block]))
        gprod = gpos * dst_vec + jnp.concatenate(negs_part, axis=0)
        v_own[t] = gprod * src_vec
        send_v()
        subl = lax.broadcasted_iota(I32, (128, 256), 0)
        s_hot = one_hot(subl == rows[0:1])
        grad_src = dot(jnp.concatenate([s_hot, s_hot], axis=1), split(gprod * rel))
        block, state = adagrad(src_blk, src_st_in[t], grad_src)
        src_new[t] = block
        src_st_new[t] = state

        send_src()
        d_hot = one_hot(subl == rows[1:2])
        n_hot = one_hot(subl == rows[3:4])
        grad_dst = dot(
            jnp.concatenate([d_hot, d_hot, n_hot, n_hot], axis=1),
            jnp.concatenate([split(gpos * a), split(jnp.concatenate(rows_part, axis=0))], axis=0),
        )
        block, state = adagrad(dst_blk, dst_st_cur[...], grad_dst)
        dst_cur[...] = block
        dst_st_cur[...] = state

    def enter():
        pl.semaphore_wait(barrier, 28)

    def first_sends():
        enter()
        state_copy(0).start()
        block_copy(0).start()
        edge_copy(1, EDGES_1).start()
        edge_copy(2, EDGES_2).start()
        sib_idx_copy(0).start()
        v_copy(0).start()

    gather_relations(lambda e: r_smem[0, 0, e])
    work(0, lambda: None, first_sends)

    @pl.loop(1, STEPS)
    def _(t):
        edge_copy(t, EDGES_1).wait()
        sib_idx_copy(t).start()
        load = pltpu.make_async_copy(idx.at[t], idx_smem.at[t], smem_sem)
        load.start()
        load.wait()
        gather_relations(lambda e: idx_smem[t, 2, e])
        sib_idx_copy(t - 1).wait()
        v_copy(t - 1).wait()
        for c in range(3):
            add_third(t - 1, c)
        state_copy(t - 1).wait()
        block_copy(t - 1).wait()

        def send_src():
            @pl.when(t < 2)
            def _():
                state_copy(t).start()
                block_copy(t).start()

            @pl.when(t == 2)
            def _():
                ends[0].start()
                ends[1].start()

        work(t, v_copy(t).start, send_src)

    ends[2].start()
    ends[3].start()

    def rows_of(c, p, j):
        if p == 2:
            return pl.ds(pl.multiple_of(lax.div(j, 2) * 8, 8), 8)
        return pl.ds(pl.multiple_of(j * CHUNK[c][p], CHUNK[c][p]), CHUNK[c][p])

    def start_phase(c, p):
        axis = ORDERS[c][p]
        source = half.at[c] if p == 0 else held[c, p - 1]

        @pl.loop(1, SIZE[axis])
        def _(o):
            target = lax.rem(me[axis] + o, SIZE[axis])
            pltpu.make_async_remote_copy(
                source.at[rows_of(c, p, target)],
                recv[c, p].at[o - 1],
                send_sem.at[c, p],
                recv_sem.at[c, p],
                device_id=partner(me, axis, o),
                device_id_type=MESH,
            ).start()

    def finish_phase(c, p):
        axis = ORDERS[c][p]
        pltpu.make_async_remote_copy(
            recv[c, p],
            recv[c, p],
            send_sem.at[c, p],
            recv_sem.at[c, p],
            device_id=sibling,
            device_id_type=MESH,
        ).wait()
        source = half.at[c] if p == 0 else held[c, p - 1]
        total = source[rows_of(c, p, me[axis]), :]
        for o in range(SIZE[axis] - 1):
            total = total + recv[c, p][o]
        return total

    sib_idx_copy(2).wait()
    v_copy(2).wait()
    for c in (2, 0, 1):
        add_third(2, c)
        start_phase(c, 0)
    last = {}
    for c, p in ROUND:
        total = finish_phase(c, p)
        if p < 2:
            held[c, p][...] = total
            start_phase(c, p + 1)
        else:
            odd = lax.rem(me[ORDERS[c][2]], 2)
            last[c] = jnp.where(odd == 0, total[0:4], total[4:8])
    grad = jnp.concatenate([last[0], last[1], last[2]], axis=1)
    owner = lax.axis_index("src") * 32 + lax.axis_index("dst")
    near = table[pl.ds(pl.multiple_of(lax.div(owner, 2) * 8, 8), 8), :]
    own = jnp.where(lax.rem(owner, 2) == 0, near[0:4], near[4:8])
    state = as_column(rel_st[...]) + jnp.sum(grad * grad, axis=1, keepdims=True) * (1.0 / 384)
    rel_st_out[...] = as_row(state)
    rel_out[...] = own - 0.1 * grad / jnp.sqrt(state)
    for copy in ends:
        copy.wait()


def store_kernel(*refs):
    sources, targets, held, sems = refs[:6], refs[6:12], refs[12:18], refs[18]
    loads = [pltpu.make_async_copy(sources[i], held[i], sems.at[0, i]) for i in range(6)]
    stores = [pltpu.make_async_copy(held[i], targets[i], sems.at[1, i]) for i in range(6)]
    for load in loads:
        load.start()
    for load, store in zip(loads, stores):
        load.wait()
        store.start()
    for store in stores:
        store.wait()


def on_device(
    source_embedding_table,
    source_adagrad_state,
    destination_embedding_table,
    destination_adagrad_state,
    relations,
    rel_state,
    source_edge_rows,
    destination_edge_rows,
    edge_relation_index,
    negative_block_rows,
    bucket_block_counts,
):
    vmem, hbm = pl.BlockSpec(memory_space=pltpu.VMEM), pl.BlockSpec(memory_space=pl.ANY)
    dma = pltpu.SemaphoreType.DMA
    scratch = [
        pltpu.VMEM((2048, 384), F32),
        pltpu.VMEM((1, 4), F32),
        pltpu.VMEM((3, 1, 256), I32),
        pltpu.VMEM((3, 1, 256), I32),
        pltpu.VMEM((3, 1, 256), I32),
        pltpu.VMEM((3, 2, 128), I32),
        pltpu.SMEM((3, 1, 256), I32),
        pltpu.SMEM((1, 3), I32),
        pltpu.VMEM((3, 8, 256), I32),
        pltpu.VMEM((3, 8, 256), I32),
        pltpu.VMEM((3, 8, 256), I32),
        pltpu.SMEM((3, 8, 256), I32),
        pltpu.VMEM((3, 128, 384), F32),
        pltpu.VMEM((3, 1, 128), F32),
        pltpu.VMEM((3, 128, 384), F32),
        pltpu.VMEM((3, 1, 128), F32),
        pltpu.VMEM((128, 384), F32),
        pltpu.VMEM((1, 128), F32),
        pltpu.VMEM((256, 384), F32),
        pltpu.VMEM((3, 256, 384), F32),
        pltpu.VMEM((3, 256, 384), F32),
        pltpu.VMEM((3, 1024, 128), F32),
    ]
    for c in range(3):
        for p in range(3):
            scratch.append(pltpu.VMEM((SIZE[ORDERS[c][p]] - 1, CHUNK[c][p], 128), F32))
    for c in range(3):
        for p in range(2):
            scratch.append(pltpu.VMEM((CHUNK[c][p], 128), F32))
    scratch += [dma((12,)), dma, dma((3, 2)), dma((3, 2)), dma((2, 2)), dma((2, 2)), dma((3, 2)), dma((4, 2))]
    scratch += [dma((3, 3)), dma((3, 3))]
    block = jax.ShapeDtypeStruct((128, 384), F32)
    row = jax.ShapeDtypeStruct((1, 128), F32)
    results = (block, row, block, row)
    results += (jax.ShapeDtypeStruct((4, 384), F32), jax.ShapeDtypeStruct((1, 4), F32))
    outs = pl.pallas_call(
        window_kernel,
        out_shape=results,
        in_specs=[hbm] * 11,
        out_specs=(vmem,) * 6,
        scratch_shapes=scratch,
        compiler_params=pltpu.CompilerParams(
            collective_id=0, has_side_effects=True, vmem_limit_bytes=VMEM_LIMIT
        ),
    )(
        source_embedding_table[0, 0],
        source_adagrad_state[0],
        destination_embedding_table[0, 0],
        destination_adagrad_state[0],
        relations,
        rel_state[None],
        source_edge_rows.reshape(STEPS, 1, 256),
        destination_edge_rows.reshape(STEPS, 1, 256),
        edge_relation_index.reshape(STEPS, 1, 256),
        negative_block_rows[0, 0],
        bucket_block_counts[0],
    )
    src_out, src_st, dst_out, dst_st, rel_out, rel_st = pl.pallas_call(
        store_kernel,
        out_shape=results,
        in_specs=[hbm] * 6,
        out_specs=(hbm,) * 6,
        scratch_shapes=[pltpu.VMEM(r.shape, F32) for r in results] + [dma((2, 6))],
        compiler_params=pltpu.CompilerParams(vmem_limit_bytes=VMEM_LIMIT),
    )(*outs)
    return (
        src_out[None, None],
        src_st[None],
        dst_out[None, None],
        dst_st[None],
        rel_out,
        rel_st[0],
    )


def solution(mesh):
    in_specs = (
        P("src", "dst", None, None),
        P("src", "dst", None),
        P("src", "dst", None, None),
        P("src", "dst", None),
        P(),
        P(("src", "dst")),
        P("src", "dst", None, None),
        P("src", "dst", None, None),
        P("src", "dst", None, None),
        P("src", "dst", None, None, None),
        P("src", "dst", None),
    )
    out_specs = (
        P("src", "dst", None, None),
        P("src", "dst", None),
        P("src", "dst", None, None),
        P("src", "dst", None),
        P(("src", "dst"), None),
        P(("src", "dst")),
    )
    return jax.shard_map(
        on_device, mesh=mesh, in_specs=in_specs, out_specs=out_specs, check_vma=False
    )
```

```python
import jax
import jax.numpy as jnp
from jax import lax
from jax.experimental import pallas as pl
from jax.experimental.pallas import tpu as pltpu
from jax.sharding import PartitionSpec as P

MESH = pl.DeviceIdType.MESH
F32, BF16, I32 = jnp.float32, jnp.bfloat16, jnp.int32
ORDERS = (("z", "y"), ("y", "z"), ("z", "y"))
SIZE = {"x": 4, "y": 8, "z": 8}
THIRDS = (0, 2, 1)
STEPS = 3
VMEM_LIMIT = 60 * 2**20
EDGES_1, EDGES_2, NEXT, SRC_END, DST_END = (0, 31), (0, 30), (1, 31), (1, 2), (0, 3)


def coords():
    s, d = lax.axis_index("src"), lax.axis_index("dst")
    return {
        "core": lax.rem(s, 2),
        "x": lax.rem(lax.div(s, 2), 4),
        "y": lax.div(s, 8) * 4 + lax.rem(d, 4),
        "z": lax.div(d, 4),
    }


def device_of(at):
    return (
        lax.div(at["y"], 4) * 8 + at["x"] * 2 + at["core"],
        at["z"] * 4 + lax.rem(at["y"], 4),
    )


def partner(me, axis, offset):
    return device_of({**me, axis: lax.rem(me[axis] + offset, SIZE[axis])})


def moved(offset):
    s, d = lax.axis_index("src"), lax.axis_index("dst")
    return (lax.rem(s + offset[0], 16), lax.rem(d + offset[1], 32))


def dot(a, b):
    return jnp.dot(a, b, preferred_element_type=F32)


def dot_nt(a, b):
    return lax.dot_general(a, b, (((1,), (1,)), ((), ())), preferred_element_type=F32)


def one_hot(mask):
    return jnp.where(mask, 1.0, 0.0).astype(BF16)


def split(value, axis=0):
    high = value.astype(BF16)
    low = (value - high.astype(F32)).astype(BF16)
    return jnp.concatenate([high, low], axis=axis)


def sigmoid(value):
    return 1.0 / (1.0 + jnp.exp(-value))


def eye(n):
    return lax.broadcasted_iota(I32, (n, n), 0) == lax.broadcasted_iota(I32, (n, n), 1)


def as_column(row):
    return jnp.sum(jnp.where(eye(row.shape[1]), row, 0.0), axis=1, keepdims=True)


def as_row(column):
    return jnp.sum(jnp.where(eye(column.shape[0]), column, 0.0), axis=0, keepdims=True)


def adagrad(block, state_row, grad):
    state = as_column(state_row) + jnp.sum(grad * grad, axis=1, keepdims=True) * (1.0 / 384)
    return block - 0.1 * grad / jnp.sqrt(state), as_row(state)


def positions(r, c):
    k, z, x = r & 3, (r >> 4) & 7, (r >> 8) & 3
    y = ((r >> 10) << 2) | ((r >> 2) & 3)
    near, far = (z, y) if ORDERS[c][0] == "z" else (y, z)
    return (((x * 8 + near) * 8 + far) * 4) + k


def window_kernel(
    src_hbm, src_st_hbm, dst_hbm, dst_st_hbm, rel_hbm, rel_st_hbm, s_hbm, d_hbm, r_hbm, n_hbm, count_hbm,
    src_out, src_st_out, dst_out, dst_st_out, rel_out, rel_st_out,
    table, rel_st, s_raw, d_raw, r_raw, n_raw, r_smem, count_smem,
    idx_mine, idx, idx_sib, idx_smem, src_in, src_st_in, src_new, src_st_new, dst_cur, dst_st_cur,
    rel_vec, v_own, v_sib, half, *rest,
):
    relay_in, near_in, recv, held = rest[0], rest[1], rest[2:4], rest[4:6]
    (load_sem, smem_sem, idx_sem, sib_idx_sem, block_sem, state_sem, v_sem, end_sem,
     x_sem, ring_sem) = rest[6:]
    me = coords()
    sibling = device_of({**me, "core": 1 - me["core"]})

    loads = [
        pltpu.make_async_copy(source, target, load_sem.at[i])
        for i, (source, target) in enumerate(
            [
                (r_hbm, r_smem), (count_hbm, count_smem), (rel_hbm, table),
                (s_hbm, s_raw), (d_hbm, d_raw), (r_hbm, r_raw), (n_hbm, n_raw),
                (src_hbm, src_in.at[0]), (dst_hbm, dst_cur),
                (src_st_hbm, src_st_in.at[0]), (dst_st_hbm, dst_st_cur), (rel_st_hbm, rel_st),
            ]
        )
    ]
    for load in loads:
        load.start()

    barrier = pltpu.get_barrier_semaphore()
    pl.semaphore_signal(barrier, inc=1, device_id=sibling, device_id_type=MESH)
    for ds, dd in (NEXT, EDGES_1, EDGES_2, SRC_END, DST_END):
        for offset in ((ds, dd), ((16 - ds) % 16, (32 - dd) % 32)):
            pl.semaphore_signal(barrier, inc=1, device_id=moved(offset), device_id_type=MESH)

    for axis in "xyz":

        @pl.loop(1, SIZE[axis])
        def _(o):
            pl.semaphore_signal(
                barrier, inc=1, device_id=partner(me, axis, o), device_id_type=MESH
            )

    half[...] = jnp.zeros_like(half)
    for load in loads:
        load.wait()
    block_of = lax.broadcasted_iota(I32, (1, 256), 1) >> 7
    for t in range(STEPS):
        idx_mine[t, 0:1, :] = s_raw[t]
        idx_mine[t, 1:2, :] = d_raw[t]
        idx_mine[t, 2:3, :] = r_raw[t]
        idx_mine[t, 3:4, 0:128] = n_raw[t, 0:1, :]
        idx_mine[t, 3:4, 128:256] = n_raw[t, 1:2, :]
        live = jnp.where(block_of < count_smem[0, t], 1, 0)
        idx_mine[t, 4:8, :] = jnp.broadcast_to(live, (4, 256))
    idx[0] = idx_mine[0]

    def remote(source, target, sems, to):
        return pltpu.make_async_remote_copy(
            source, target, sems.at[0], sems.at[1], device_id=to, device_id_type=MESH
        )

    def edge_copy(t, offset):
        return remote(idx_mine.at[t], idx.at[t], idx_sem.at[t], moved(offset))

    def sib_idx_copy(t):
        return remote(idx.at[t], idx_sib.at[t], sib_idx_sem.at[t], sibling)

    def v_copy(t):
        return remote(v_own.at[t], v_sib.at[t], v_sem.at[t], sibling)

    def block_copy(t):
        return remote(src_new.at[t], src_in.at[t + 1], block_sem.at[t], moved(NEXT))

    def state_copy(t):
        return remote(src_st_new.at[t], src_st_in.at[t + 1], state_sem.at[t], moved(NEXT))

    ends = [
        remote(src_st_new.at[2], src_st_out, end_sem.at[0], moved(SRC_END)),
        remote(src_new.at[2], src_out, end_sem.at[1], moved(SRC_END)),
        remote(dst_st_cur, dst_st_out, end_sem.at[2], moved(DST_END)),
        remote(dst_cur, dst_out, end_sem.at[3], moved(DST_END)),
    ]

    def gather_relations(row_of):
        @pl.loop(0, 32)
        def _(i):
            for j in range(8):
                e = i * 8 + j
                rel_vec[pl.ds(e, 1), :] = table[pl.ds(row_of(e), 1), :]

    def add_third(t, c):
        v = jnp.concatenate(
            [v_own[t, :, c * 128 : (c + 1) * 128], v_sib[t, :, c * 128 : (c + 1) * 128]], axis=0
        )
        rhs = split(v, axis=1)
        r = jnp.concatenate([idx[t, 2:3, :], idx_sib[t, 2:3, :]], axis=1)
        at = jnp.where(((r >> 7) & 1) == me["core"], positions(r, c), -1)

        @pl.loop(0, 4)
        def _(ch):
            rows = pl.ds(pl.multiple_of(ch * 256, 256), 256)
            hot = one_hot(lax.broadcasted_iota(I32, (256, 512), 0) + ch * 256 == at)
            both = dot(hot, rhs)
            half[c, rows, :] += both[:, :128] + both[:, 128:]

    def work(t, send_v, send_src):
        rows = idx[t]
        columns = jnp.transpose(rows.astype(F32)).astype(I32)
        s_col, d_col, n_col = columns[:, 0:1], columns[:, 1:2], columns[:, 3:4]
        live = columns[:, 4:5].astype(F32)
        lanes = lax.broadcasted_iota(I32, (256, 256), 1) & 127
        src_blk, dst_blk = src_in[t], dst_cur[...]
        dst_two = split(dst_blk)
        src_vec = dot(one_hot(lanes == s_col), split(src_blk))
        dst_vec = dot(one_hot(lanes == d_col), dst_two)
        negb = dot(one_hot(lanes[:, :128] == n_col), dst_two[:128]).astype(BF16)
        rel = rel_vec[...]
        a = src_vec * rel
        ab = a.astype(BF16)
        pos = jnp.sum(a * dst_vec, axis=1, keepdims=True)
        gpos = -sigmoid(-pos) * live
        negs_part, rows_part = [], []
        for c in range(2):
            block = slice(c * 128, (c + 1) * 128)
            neg = dot_nt(ab[block], negb[block])
            gneg = sigmoid(neg) * (1.0 / 128) * live[block]
            negs_part.append(dot(gneg.astype(BF16), negb[block]))
            rows_part.append(dot(jnp.transpose(gneg).astype(BF16), ab[block]))
        gprod = gpos * dst_vec + jnp.concatenate(negs_part, axis=0)
        v_own[t] = gprod * src_vec
        send_v()
        subl = lax.broadcasted_iota(I32, (128, 256), 0)
        s_hot = one_hot(subl == rows[0:1])
        grad_src = dot(jnp.concatenate([s_hot, s_hot], axis=1), split(gprod * rel))
        block, state = adagrad(src_blk, src_st_in[t], grad_src)
        src_new[t] = block
        src_st_new[t] = state

        send_src()
        d_hot = one_hot(subl == rows[1:2])
        n_hot = one_hot(subl == rows[3:4])
        grad_dst = dot(
            jnp.concatenate([d_hot, d_hot, n_hot, n_hot], axis=1),
            jnp.concatenate([split(gpos * a), split(jnp.concatenate(rows_part, axis=0))], axis=0),
        )
        block, state = adagrad(dst_blk, dst_st_cur[...], grad_dst)
        dst_cur[...] = block
        dst_st_cur[...] = state

    def enter():
        pl.semaphore_wait(barrier, 28)

    def first_sends():
        enter()
        state_copy(0).start()
        block_copy(0).start()
        edge_copy(1, EDGES_1).start()
        edge_copy(2, EDGES_2).start()
        sib_idx_copy(0).start()
        v_copy(0).start()

    gather_relations(lambda e: r_smem[0, 0, e])
    work(0, lambda: None, first_sends)

    @pl.loop(1, STEPS)
    def _(t):
        edge_copy(t, EDGES_1).wait()
        sib_idx_copy(t).start()
        load = pltpu.make_async_copy(idx.at[t], idx_smem.at[t], smem_sem)
        load.start()
        load.wait()
        gather_relations(lambda e: idx_smem[t, 2, e])
        sib_idx_copy(t - 1).wait()
        v_copy(t - 1).wait()
        for c in range(3):
            add_third(t - 1, c)
        state_copy(t - 1).wait()
        block_copy(t - 1).wait()

        def send_src():
            @pl.when(t < 2)
            def _():
                state_copy(t).start()
                block_copy(t).start()

            @pl.when(t == 2)
            def _():
                ends[0].start()
                ends[1].start()

        work(t, v_copy(t).start, send_src)

    ends[2].start()
    ends[3].start()

    ahead, across, behind = (lax.rem(me["x"] + o, 4) for o in (1, 2, 3))

    def x_copy(c, k):
        lower, upper = 0, 128
        chunk, first, target, step = (
            (across, lower, relay_in.at[c, 0], 1),
            (across, upper, relay_in.at[c, 1], 3),
            (ahead, upper, near_in.at[c, 0], 1),
            (behind, lower, near_in.at[c, 1], 3),
            (ahead, lower, near_in.at[c, 2], 1),
            (behind, upper, near_in.at[c, 3], 3),
        )[k]
        source = half.at[c, pl.ds(pl.multiple_of(chunk * 256 + first, 128), 128)]
        return remote(source, target, x_sem.at[c, k], partner(me, "x", step))

    def ring_rows(p, j):
        if p == 1:
            return pl.ds(pl.multiple_of(lax.div(j, 2) * 8, 8), 8)
        return pl.ds(pl.multiple_of(j * 32, 32), 32)

    def ring_start(c, p):
        axis = ORDERS[c][p]
        for o in range(1, 8):
            target = lax.rem(me[axis] + o, 8)
            pltpu.make_async_remote_copy(
                held[p].at[c, ring_rows(p, target)],
                recv[p].at[c, o - 1],
                ring_sem.at[c, p, 0],
                ring_sem.at[c, p, 1],
                device_id=partner(me, axis, o),
                device_id_type=MESH,
            ).start()

    def ring_all(c, p):
        return remote(recv[p].at[c], recv[p].at[c], ring_sem.at[c, p], sibling)

    def ring_finish(c, p):
        ring_all(c, p).wait_recv()
        total = held[p][c, ring_rows(p, me[ORDERS[c][p]]), :]
        for o in range(7):
            total = total + recv[p][c, o]
        return total

    sib_idx_copy(2).wait()
    v_copy(2).wait()
    for c in THIRDS:
        add_third(2, c)
        for k in range(4):
            x_copy(c, k).start()
    for c in THIRDS:
        for k, chunk, first in ((0, ahead, 0), (1, behind, 128)):
            x_copy(c, k).wait_recv()
            rows = pl.ds(pl.multiple_of(chunk * 256 + first, 128), 128)
            half[c, rows, :] += relay_in[c, k]
            x_copy(c, 4 + k).start()
    own = pl.multiple_of(me["x"] * 256, 256)
    for c in THIRDS:
        for k in range(2, 6):
            x_copy(c, k).wait_recv()
        held[0][c, 0:128, :] = half[c, pl.ds(own, 128), :] + near_in[c, 1] + near_in[c, 2]
        held[0][c, 128:256, :] = (
            half[c, pl.ds(pl.multiple_of(own + 128, 128), 128), :] + near_in[c, 0] + near_in[c, 3]
        )
        ring_start(c, 0)
    for c in THIRDS:
        held[1][c] = ring_finish(c, 0)
        ring_start(c, 1)
    last = {}
    for c in THIRDS:
        total = ring_finish(c, 1)
        odd = lax.rem(me[ORDERS[c][1]], 2)
        last[c] = jnp.where(odd == 0, total[0:4], total[4:8])
    grad = jnp.concatenate([last[0], last[1], last[2]], axis=1)
    owner = lax.axis_index("src") * 32 + lax.axis_index("dst")
    near = table[pl.ds(pl.multiple_of(lax.div(owner, 2) * 8, 8), 8), :]
    own_rel = jnp.where(lax.rem(owner, 2) == 0, near[0:4], near[4:8])
    state = as_column(rel_st[...]) + jnp.sum(grad * grad, axis=1, keepdims=True) * (1.0 / 384)
    rel_st_out[...] = as_row(state)
    rel_out[...] = own_rel - 0.1 * grad / jnp.sqrt(state)
    for c in THIRDS:
        for k in range(6):
            x_copy(c, k).wait_send()
        for p in range(2):
            ring_all(c, p).wait_send()
    for copy in ends:
        copy.wait()


def store_kernel(*refs):
    sources, targets, held, sems = refs[:6], refs[6:12], refs[12:18], refs[18]
    loads = [pltpu.make_async_copy(sources[i], held[i], sems.at[0, i]) for i in range(6)]
    stores = [pltpu.make_async_copy(held[i], targets[i], sems.at[1, i]) for i in range(6)]
    for load in loads:
        load.start()
    for load, store in zip(loads, stores):
        load.wait()
        store.start()
    for store in stores:
        store.wait()


def on_device(
    source_embedding_table,
    source_adagrad_state,
    destination_embedding_table,
    destination_adagrad_state,
    relations,
    rel_state,
    source_edge_rows,
    destination_edge_rows,
    edge_relation_index,
    negative_block_rows,
    bucket_block_counts,
):
    vmem, hbm = pl.BlockSpec(memory_space=pltpu.VMEM), pl.BlockSpec(memory_space=pl.ANY)
    dma = pltpu.SemaphoreType.DMA
    scratch = [
        pltpu.VMEM((2048, 384), F32),
        pltpu.VMEM((1, 4), F32),
        pltpu.VMEM((3, 1, 256), I32),
        pltpu.VMEM((3, 1, 256), I32),
        pltpu.VMEM((3, 1, 256), I32),
        pltpu.VMEM((3, 2, 128), I32),
        pltpu.SMEM((3, 1, 256), I32),
        pltpu.SMEM((1, 3), I32),
        pltpu.VMEM((3, 8, 256), I32),
        pltpu.VMEM((3, 8, 256), I32),
        pltpu.VMEM((3, 8, 256), I32),
        pltpu.SMEM((3, 8, 256), I32),
        pltpu.VMEM((3, 128, 384), F32),
        pltpu.VMEM((3, 1, 128), F32),
        pltpu.VMEM((3, 128, 384), F32),
        pltpu.VMEM((3, 1, 128), F32),
        pltpu.VMEM((128, 384), F32),
        pltpu.VMEM((1, 128), F32),
        pltpu.VMEM((256, 384), F32),
        pltpu.VMEM((3, 256, 384), F32),
        pltpu.VMEM((3, 256, 384), F32),
        pltpu.VMEM((3, 1024, 128), F32),
    ]
    scratch += [
        pltpu.VMEM((3, 2, 128, 128), F32),
        pltpu.VMEM((3, 4, 128, 128), F32),
        pltpu.VMEM((3, 7, 32, 128), F32),
        pltpu.VMEM((3, 7, 8, 128), F32),
        pltpu.VMEM((3, 256, 128), F32),
        pltpu.VMEM((3, 32, 128), F32),
    ]
    scratch += [dma((12,)), dma, dma((3, 2)), dma((3, 2)), dma((2, 2)), dma((2, 2)), dma((3, 2)), dma((4, 2))]
    scratch += [dma((3, 6, 2)), dma((3, 2, 2))]
    block = jax.ShapeDtypeStruct((128, 384), F32)
    row = jax.ShapeDtypeStruct((1, 128), F32)
    results = (block, row, block, row)
    results += (jax.ShapeDtypeStruct((4, 384), F32), jax.ShapeDtypeStruct((1, 4), F32))
    outs = pl.pallas_call(
        window_kernel,
        out_shape=results,
        in_specs=[hbm] * 11,
        out_specs=(vmem,) * 6,
        scratch_shapes=scratch,
        compiler_params=pltpu.CompilerParams(
            collective_id=0, has_side_effects=True, vmem_limit_bytes=VMEM_LIMIT
        ),
    )(
        source_embedding_table[0, 0],
        source_adagrad_state[0],
        destination_embedding_table[0, 0],
        destination_adagrad_state[0],
        relations,
        rel_state[None],
        source_edge_rows.reshape(STEPS, 1, 256),
        destination_edge_rows.reshape(STEPS, 1, 256),
        edge_relation_index.reshape(STEPS, 1, 256),
        negative_block_rows[0, 0],
        bucket_block_counts[0],
    )
    src_out, src_st, dst_out, dst_st, rel_out, rel_st = pl.pallas_call(
        store_kernel,
        out_shape=results,
        in_specs=[hbm] * 6,
        out_specs=(hbm,) * 6,
        scratch_shapes=[pltpu.VMEM(r.shape, F32) for r in results] + [dma((2, 6))],
        compiler_params=pltpu.CompilerParams(vmem_limit_bytes=VMEM_LIMIT),
    )(*outs)
    return (
        src_out[None, None],
        src_st[None],
        dst_out[None, None],
        dst_st[None],
        rel_out,
        rel_st[0],
    )


def solution(mesh):
    in_specs = (
        P("src", "dst", None, None),
        P("src", "dst", None),
        P("src", "dst", None, None),
        P("src", "dst", None),
        P(),
        P(("src", "dst")),
        P("src", "dst", None, None),
        P("src", "dst", None, None),
        P("src", "dst", None, None),
        P("src", "dst", None, None, None),
        P("src", "dst", None),
    )
    out_specs = (
        P("src", "dst", None, None),
        P("src", "dst", None),
        P("src", "dst", None, None),
        P("src", "dst", None),
        P(("src", "dst"), None),
        P(("src", "dst")),
    )
    return jax.shard_map(
        on_device, mesh=mesh, in_specs=in_specs, out_specs=out_specs, check_vma=False
    )
```

```python
import jax
import jax.numpy as jnp
from jax import lax
from jax.experimental import pallas as pl
from jax.experimental.pallas import tpu as pltpu
from jax.sharding import PartitionSpec as P

MESH = pl.DeviceIdType.MESH
F32, BF16, I32 = jnp.float32, jnp.bfloat16, jnp.int32
ORDERS = (("z", "y", "x"), ("x", "y", "z"), ("x", "z", "y"))
SIZE = {"x": 4, "y": 8, "z": 8}
THIRDS = (0, 2, 1)
ALONG_X = (2, 1)
STEPS = 3
VMEM_LIMIT = 60 * 2**20
EDGES_1, EDGES_2, NEXT, SRC_END, DST_END = (0, 31), (0, 30), (1, 31), (1, 2), (0, 3)


def coords():
    s, d = lax.axis_index("src"), lax.axis_index("dst")
    return {
        "core": lax.rem(s, 2),
        "x": lax.rem(lax.div(s, 2), 4),
        "y": lax.div(s, 8) * 4 + lax.rem(d, 4),
        "z": lax.div(d, 4),
    }


def device_of(at):
    return (
        lax.div(at["y"], 4) * 8 + at["x"] * 2 + at["core"],
        at["z"] * 4 + lax.rem(at["y"], 4),
    )


def partner(me, axis, offset):
    return device_of({**me, axis: lax.rem(me[axis] + offset, SIZE[axis])})


def moved(offset):
    s, d = lax.axis_index("src"), lax.axis_index("dst")
    return (lax.rem(s + offset[0], 16), lax.rem(d + offset[1], 32))


def dot(a, b):
    return jnp.dot(a, b, preferred_element_type=F32)


def dot_nt(a, b):
    return lax.dot_general(a, b, (((1,), (1,)), ((), ())), preferred_element_type=F32)


def one_hot(mask):
    return jnp.where(mask, 1.0, 0.0).astype(BF16)


def split(value, axis=0):
    high = value.astype(BF16)
    low = (value - high.astype(F32)).astype(BF16)
    return jnp.concatenate([high, low], axis=axis)


def sigmoid(value):
    return 1.0 / (1.0 + jnp.exp(-value))


def eye(n):
    return lax.broadcasted_iota(I32, (n, n), 0) == lax.broadcasted_iota(I32, (n, n), 1)


def as_column(row):
    return jnp.sum(jnp.where(eye(row.shape[1]), row, 0.0), axis=1, keepdims=True)


def as_row(column):
    return jnp.sum(jnp.where(eye(column.shape[0]), column, 0.0), axis=0, keepdims=True)


def adagrad(block, state_row, grad):
    state = as_column(state_row) + jnp.sum(grad * grad, axis=1, keepdims=True) * (1.0 / 384)
    return block - 0.1 * grad / jnp.sqrt(state), as_row(state)


def positions(r, c):
    k, z, x = r & 3, (r >> 4) & 7, (r >> 8) & 3
    y = ((r >> 10) << 2) | ((r >> 2) & 3)
    at = {"x": x, "y": y, "z": z}
    first, second, third = ORDERS[c]
    return ((at[first] * SIZE[second] + at[second]) * SIZE[third] + at[third]) * 4 + k


def window_kernel(
    src_hbm, src_st_hbm, dst_hbm, dst_st_hbm, rel_hbm, rel_st_hbm, s_hbm, d_hbm, r_hbm, n_hbm, count_hbm,
    src_out, src_st_out, dst_out, dst_st_out, rel_out, rel_st_out,
    table, rel_st, s_raw, d_raw, r_raw, n_raw, r_smem, count_smem,
    idx_mine, idx, idx_sib, idx_smem, src_in, src_st_in, src_new, src_st_new, dst_cur, dst_st_cur,
    rel_vec, v_own, v_sib, half, *rest,
):
    relay_in, near_in, recv, held = rest[0], rest[1], rest[2:4], rest[4:6]
    z_relay, z_part, z_near = rest[6:9]
    (load_sem, smem_sem, idx_sem, sib_idx_sem, block_sem, state_sem, v_sem, end_sem,
     x_sem, z_sem, ring_sem) = rest[9:]
    me = coords()
    sibling = device_of({**me, "core": 1 - me["core"]})

    loads = [
        pltpu.make_async_copy(source, target, load_sem.at[i])
        for i, (source, target) in enumerate(
            [
                (r_hbm, r_smem), (count_hbm, count_smem), (rel_hbm, table),
                (s_hbm, s_raw), (d_hbm, d_raw), (r_hbm, r_raw), (n_hbm, n_raw),
                (src_hbm, src_in.at[0]), (dst_hbm, dst_cur),
                (src_st_hbm, src_st_in.at[0]), (dst_st_hbm, dst_st_cur), (rel_st_hbm, rel_st),
            ]
        )
    ]
    for load in loads:
        load.start()

    barrier = pltpu.get_barrier_semaphore()
    pl.semaphore_signal(barrier, inc=1, device_id=sibling, device_id_type=MESH)
    for ds, dd in (NEXT, EDGES_1, EDGES_2, SRC_END, DST_END):
        for offset in ((ds, dd), ((16 - ds) % 16, (32 - dd) % 32)):
            pl.semaphore_signal(barrier, inc=1, device_id=moved(offset), device_id_type=MESH)

    for axis in "xyz":

        @pl.loop(1, SIZE[axis])
        def _(o):
            pl.semaphore_signal(
                barrier, inc=1, device_id=partner(me, axis, o), device_id_type=MESH
            )

    half[...] = jnp.zeros_like(half)
    for load in loads:
        load.wait()
    block_of = lax.broadcasted_iota(I32, (1, 256), 1) >> 7
    for t in range(STEPS):
        idx_mine[t, 0:1, :] = s_raw[t]
        idx_mine[t, 1:2, :] = d_raw[t]
        idx_mine[t, 2:3, :] = r_raw[t]
        idx_mine[t, 3:4, 0:128] = n_raw[t, 0:1, :]
        idx_mine[t, 3:4, 128:256] = n_raw[t, 1:2, :]
        live = jnp.where(block_of < count_smem[0, t], 1, 0)
        idx_mine[t, 4:8, :] = jnp.broadcast_to(live, (4, 256))
    idx[0] = idx_mine[0]

    def remote(source, target, sems, to):
        return pltpu.make_async_remote_copy(
            source, target, sems.at[0], sems.at[1], device_id=to, device_id_type=MESH
        )

    def edge_copy(t, offset):
        return remote(idx_mine.at[t], idx.at[t], idx_sem.at[t], moved(offset))

    def sib_idx_copy(t):
        return remote(idx.at[t], idx_sib.at[t], sib_idx_sem.at[t], sibling)

    def v_copy(t, c):
        return remote(v_own.at[t, c], v_sib.at[t, c], v_sem.at[t, c], sibling)

    def send_v(t):
        for c in THIRDS:
            v_copy(t, c).start()

    def block_copy(t):
        return remote(src_new.at[t], src_in.at[t + 1], block_sem.at[t], moved(NEXT))

    def state_copy(t):
        return remote(src_st_new.at[t], src_st_in.at[t + 1], state_sem.at[t], moved(NEXT))

    ends = [
        remote(src_st_new.at[2], src_st_out, end_sem.at[0], moved(SRC_END)),
        remote(src_new.at[2], src_out, end_sem.at[1], moved(SRC_END)),
        remote(dst_st_cur, dst_st_out, end_sem.at[2], moved(DST_END)),
        remote(dst_cur, dst_out, end_sem.at[3], moved(DST_END)),
    ]

    def gather_relations(row_of):
        @pl.loop(0, 32)
        def _(i):
            for j in range(8):
                e = i * 8 + j
                rel_vec[pl.ds(e, 1), :] = table[pl.ds(row_of(e), 1), :]

    def add_third(t, c):
        v = jnp.concatenate(
            [v_own[t, c], v_sib[t, c]], axis=0
        )
        rhs = split(v, axis=1)
        r = jnp.concatenate([idx[t, 2:3, :], idx_sib[t, 2:3, :]], axis=1)
        at = jnp.where(((r >> 7) & 1) == me["core"], positions(r, c), -1)

        @pl.loop(0, 4)
        def _(ch):
            rows = pl.ds(pl.multiple_of(ch * 256, 256), 256)
            hot = one_hot(lax.broadcasted_iota(I32, (256, 512), 0) + ch * 256 == at)
            both = dot(hot, rhs)
            half[c, rows, :] += both[:, :128] + both[:, 128:]

    def work(t, send_values, send_src):
        rows = idx[t]
        columns = jnp.transpose(rows.astype(F32)).astype(I32)
        s_col, d_col, n_col = columns[:, 0:1], columns[:, 1:2], columns[:, 3:4]
        live = columns[:, 4:5].astype(F32)
        lanes = lax.broadcasted_iota(I32, (256, 256), 1) & 127
        src_blk, dst_blk = src_in[t], dst_cur[...]
        dst_two = split(dst_blk)
        src_vec = dot(one_hot(lanes == s_col), split(src_blk))
        dst_vec = dot(one_hot(lanes == d_col), dst_two)
        negb = dot(one_hot(lanes[:, :128] == n_col), dst_two[:128]).astype(BF16)
        rel = rel_vec[...]
        a = src_vec * rel
        ab = a.astype(BF16)
        pos = jnp.sum(a * dst_vec, axis=1, keepdims=True)
        gpos = -sigmoid(-pos) * live
        negs_part, rows_part = [], []
        for c in range(2):
            block = slice(c * 128, (c + 1) * 128)
            neg = dot_nt(ab[block], negb[block])
            gneg = sigmoid(neg) * (1.0 / 128) * live[block]
            negs_part.append(dot(gneg.astype(BF16), negb[block]))
            rows_part.append(dot(jnp.transpose(gneg).astype(BF16), ab[block]))
        gprod = gpos * dst_vec + jnp.concatenate(negs_part, axis=0)
        v = gprod * src_vec
        for c in range(3):
            v_own[t, c] = v[:, c * 128 : (c + 1) * 128]
        send_values()
        subl = lax.broadcasted_iota(I32, (128, 256), 0)
        s_hot = one_hot(subl == rows[0:1])
        grad_src = dot(jnp.concatenate([s_hot, s_hot], axis=1), split(gprod * rel))
        block, state = adagrad(src_blk, src_st_in[t], grad_src)
        src_new[t] = block
        src_st_new[t] = state

        send_src()
        d_hot = one_hot(subl == rows[1:2])
        n_hot = one_hot(subl == rows[3:4])
        grad_dst = dot(
            jnp.concatenate([d_hot, d_hot, n_hot, n_hot], axis=1),
            jnp.concatenate([split(gpos * a), split(jnp.concatenate(rows_part, axis=0))], axis=0),
        )
        block, state = adagrad(dst_blk, dst_st_cur[...], grad_dst)
        dst_cur[...] = block
        dst_st_cur[...] = state

    def enter():
        pl.semaphore_wait(barrier, 28)

    def first_sends():
        enter()
        state_copy(0).start()
        block_copy(0).start()
        edge_copy(1, EDGES_1).start()
        edge_copy(2, EDGES_2).start()
        sib_idx_copy(0).start()
        send_v(0)

    gather_relations(lambda e: r_smem[0, 0, e])
    work(0, lambda: None, first_sends)

    @pl.loop(1, STEPS)
    def _(t):
        edge_copy(t, EDGES_1).wait()
        sib_idx_copy(t).start()
        load = pltpu.make_async_copy(idx.at[t], idx_smem.at[t], smem_sem)
        load.start()
        load.wait()
        gather_relations(lambda e: idx_smem[t, 2, e])
        state_copy(t - 1).wait()
        block_copy(t - 1).wait()

        def send_src():
            @pl.when(t < 2)
            def _():
                state_copy(t).start()
                block_copy(t).start()

            @pl.when(t == 2)
            def _():
                ends[0].start()
                ends[1].start()

        work(t, lambda: send_v(t), send_src)

        @pl.when(t == 2)
        def _():
            ends[2].start()
            ends[3].start()

        sib_idx_copy(t - 1).wait()
        for c in THIRDS:
            v_copy(t - 1, c).wait()
            add_third(t - 1, c)

    ahead, across, behind = (lax.rem(me["x"] + o, 4) for o in (1, 2, 3))

    def x_copy(c, k):
        lower, upper = 0, 128
        chunk, first, target, step = (
            (across, lower, relay_in.at[c, 0], 1),
            (across, upper, relay_in.at[c, 1], 3),
            (ahead, upper, near_in.at[c, 0], 1),
            (behind, lower, near_in.at[c, 1], 3),
            (ahead, lower, near_in.at[c, 2], 1),
            (behind, upper, near_in.at[c, 3], 3),
        )[k]
        source = half.at[c, pl.ds(pl.multiple_of(chunk * 256 + first, 128), 128)]
        return remote(source, target, x_sem.at[c, k], partner(me, "x", step))

    z_at = [lax.rem(me["z"] + o, 8) for o in range(8)]

    def z_rows(chunk, first, count):
        return pl.ds(pl.multiple_of(z_at[chunk] * 128 + first, count), count)

    def z_copy(k):
        chunk, first, count, target, step = (
            (3, 0, 128, z_relay.at[0], 1),
            (5, 0, 128, z_relay.at[1], 7),
            (4, 0, 64, z_part.at[0], 2),
            (4, 64, 64, z_part.at[1], 6),
            (1, 0, 128, z_near.at[0], 1),
            (7, 0, 128, z_near.at[1], 7),
            (2, 0, 128, z_near.at[2], 2),
            (6, 0, 128, z_near.at[3], 6),
        )[k]
        return remote(
            half.at[0, z_rows(chunk, first, count)], target, z_sem.at[k], partner(me, "z", step)
        )

    def ring_rows(c, p, j):
        if p == 1:
            return pl.ds(pl.multiple_of(lax.div(j, 2) * 8, 8), 8)
        count = 16 if c == 0 else 32
        return pl.ds(pl.multiple_of(j * count, count), count)

    def ring_in(c, p):
        return recv[p].at[c, 0 : SIZE[ORDERS[c][p + 1]] - 1, 0 : (8 if p else 16 if c == 0 else 32)]

    def ring_start(c, p):
        axis = ORDERS[c][p + 1]
        for o in range(1, SIZE[axis]):
            target = lax.rem(me[axis] + o, SIZE[axis])
            pltpu.make_async_remote_copy(
                held[p].at[c, ring_rows(c, p, target)],
                ring_in(c, p).at[o - 1],
                ring_sem.at[c, p, 0],
                ring_sem.at[c, p, 1],
                device_id=partner(me, axis, o),
                device_id_type=MESH,
            ).start()

    def ring_all(c, p):
        return remote(ring_in(c, p), ring_in(c, p), ring_sem.at[c, p], sibling)

    def ring_finish(c, p):
        axis = ORDERS[c][p + 1]
        ring_all(c, p).wait_recv()
        total = held[p][c, ring_rows(c, p, me[axis]), :]
        count = total.shape[0]
        for o in range(SIZE[axis] - 1):
            total = total + recv[p][c, o, 0:count]
        return total

    sib_idx_copy(2).wait()
    for c in THIRDS:
        v_copy(2, c).wait()
        add_third(2, c)
        if c == 0:
            for k in range(6):
                z_copy(k).start()
        else:
            for k in range(4):
                x_copy(c, k).start()

    def relay_x(c):
        for k, chunk, first in ((0, ahead, 0), (1, behind, 128)):
            x_copy(c, k).wait_recv()
            rows = pl.ds(pl.multiple_of(chunk * 256 + first, 128), 128)
            half[c, rows, :] += relay_in[c, k]
            x_copy(c, 4 + k).start()

    def relay_z():
        for k, chunk, first in ((0, 2, 0), (1, 6, 64)):
            z_copy(k).wait_recv()
            half[0, z_rows(chunk, 0, 128), :] += z_relay[k]
            z_copy(2 + k).wait_recv()
            half[0, z_rows(chunk, first, 64), :] += z_part[k]
            z_copy(6 + k).start()

    relay_x(2)
    relay_z()
    relay_x(1)
    own = pl.multiple_of(me["x"] * 256, 256)

    def finish_x(c):
        for k in range(2, 6):
            x_copy(c, k).wait_recv()
        held[0][c, 0:128, :] = half[c, pl.ds(own, 128), :] + near_in[c, 1] + near_in[c, 2]
        held[0][c, 128:256, :] = (
            half[c, pl.ds(pl.multiple_of(own + 128, 128), 128), :] + near_in[c, 0] + near_in[c, 3]
        )
        ring_start(c, 0)

    def finish_z():
        for k in range(4, 8):
            z_copy(k).wait_recv()
        total = half[0, z_rows(0, 0, 128), :]
        for k in range(4):
            total = total + z_near[k]
        held[0][0, 0:128, :] = total
        ring_start(0, 0)

    finish_x(2)
    finish_z()
    finish_x(1)
    for c in (2, 0, 1):
        total = ring_finish(c, 0)
        held[1][c, 0 : total.shape[0], :] = total
        ring_start(c, 1)
    last = {}
    for c in (2, 0, 1):
        total = ring_finish(c, 1)
        odd = lax.rem(me[ORDERS[c][2]], 2)
        last[c] = jnp.where(odd == 0, total[0:4], total[4:8])
    grad = jnp.concatenate([last[0], last[1], last[2]], axis=1)
    owner = lax.axis_index("src") * 32 + lax.axis_index("dst")
    near = table[pl.ds(pl.multiple_of(lax.div(owner, 2) * 8, 8), 8), :]
    own_rel = jnp.where(lax.rem(owner, 2) == 0, near[0:4], near[4:8])
    state = as_column(rel_st[...]) + jnp.sum(grad * grad, axis=1, keepdims=True) * (1.0 / 384)
    rel_st_out[...] = as_row(state)
    rel_out[...] = own_rel - 0.1 * grad / jnp.sqrt(state)
    for k in range(8):
        z_copy(k).wait_send()
    for c in ALONG_X:
        for k in range(6):
            x_copy(c, k).wait_send()
    for c in THIRDS:
        for p in range(2):
            ring_all(c, p).wait_send()
    for copy in ends:
        copy.wait()


def store_kernel(*refs):
    sources, targets, held, sems = refs[:6], refs[6:12], refs[12:18], refs[18]
    loads = [pltpu.make_async_copy(sources[i], held[i], sems.at[0, i]) for i in range(6)]
    stores = [pltpu.make_async_copy(held[i], targets[i], sems.at[1, i]) for i in range(6)]
    for load in loads:
        load.start()
    for load, store in zip(loads, stores):
        load.wait()
        store.start()
    for store in stores:
        store.wait()


def on_device(
    source_embedding_table,
    source_adagrad_state,
    destination_embedding_table,
    destination_adagrad_state,
    relations,
    rel_state,
    source_edge_rows,
    destination_edge_rows,
    edge_relation_index,
    negative_block_rows,
    bucket_block_counts,
):
    vmem, hbm = pl.BlockSpec(memory_space=pltpu.VMEM), pl.BlockSpec(memory_space=pl.ANY)
    dma = pltpu.SemaphoreType.DMA
    scratch = [
        pltpu.VMEM((2048, 384), F32),
        pltpu.VMEM((1, 4), F32),
        pltpu.VMEM((3, 1, 256), I32),
        pltpu.VMEM((3, 1, 256), I32),
        pltpu.VMEM((3, 1, 256), I32),
        pltpu.VMEM((3, 2, 128), I32),
        pltpu.SMEM((3, 1, 256), I32),
        pltpu.SMEM((1, 3), I32),
        pltpu.VMEM((3, 8, 256), I32),
        pltpu.VMEM((3, 8, 256), I32),
        pltpu.VMEM((3, 8, 256), I32),
        pltpu.SMEM((3, 8, 256), I32),
        pltpu.VMEM((3, 128, 384), F32),
        pltpu.VMEM((3, 1, 128), F32),
        pltpu.VMEM((3, 128, 384), F32),
        pltpu.VMEM((3, 1, 128), F32),
        pltpu.VMEM((128, 384), F32),
        pltpu.VMEM((1, 128), F32),
        pltpu.VMEM((256, 384), F32),
        pltpu.VMEM((3, 3, 256, 128), F32),
        pltpu.VMEM((3, 3, 256, 128), F32),
        pltpu.VMEM((3, 1024, 128), F32),
    ]
    scratch += [
        pltpu.VMEM((3, 2, 128, 128), F32),
        pltpu.VMEM((3, 4, 128, 128), F32),
        pltpu.VMEM((3, 7, 32, 128), F32),
        pltpu.VMEM((3, 7, 8, 128), F32),
        pltpu.VMEM((3, 256, 128), F32),
        pltpu.VMEM((3, 32, 128), F32),
        pltpu.VMEM((2, 128, 128), F32),
        pltpu.VMEM((2, 64, 128), F32),
        pltpu.VMEM((4, 128, 128), F32),
    ]
    scratch += [dma((12,)), dma, dma((3, 2)), dma((3, 2)), dma((2, 2)), dma((2, 2)), dma((3, 3, 2)), dma((4, 2))]
    scratch += [dma((3, 6, 2)), dma((8, 2)), dma((3, 2, 2))]
    block = jax.ShapeDtypeStruct((128, 384), F32)
    row = jax.ShapeDtypeStruct((1, 128), F32)
    results = (block, row, block, row)
    results += (jax.ShapeDtypeStruct((4, 384), F32), jax.ShapeDtypeStruct((1, 4), F32))
    outs = pl.pallas_call(
        window_kernel,
        out_shape=results,
        in_specs=[hbm] * 11,
        out_specs=(hbm,) * 4 + (vmem,) * 2,
        scratch_shapes=scratch,
        compiler_params=pltpu.CompilerParams(
            collective_id=0, has_side_effects=True, vmem_limit_bytes=VMEM_LIMIT
        ),
    )(
        source_embedding_table[0, 0],
        source_adagrad_state[0],
        destination_embedding_table[0, 0],
        destination_adagrad_state[0],
        relations,
        rel_state[None],
        source_edge_rows.reshape(STEPS, 1, 256),
        destination_edge_rows.reshape(STEPS, 1, 256),
        edge_relation_index.reshape(STEPS, 1, 256),
        negative_block_rows[0, 0],
        bucket_block_counts[0],
    )
    src_out, src_st, dst_out, dst_st, rel_out, rel_st = pl.pallas_call(
        store_kernel,
        out_shape=results,
        in_specs=[hbm] * 6,
        out_specs=(hbm,) * 6,
        scratch_shapes=[pltpu.VMEM(r.shape, F32) for r in results] + [dma((2, 6))],
        compiler_params=pltpu.CompilerParams(vmem_limit_bytes=VMEM_LIMIT),
    )(*outs)
    return (
        src_out[None, None],
        src_st[None],
        dst_out[None, None],
        dst_st[None],
        rel_out,
        rel_st[0],
    )


def solution(mesh):
    in_specs = (
        P("src", "dst", None, None),
        P("src", "dst", None),
        P("src", "dst", None, None),
        P("src", "dst", None),
        P(),
        P(("src", "dst")),
        P("src", "dst", None, None),
        P("src", "dst", None, None),
        P("src", "dst", None, None),
        P("src", "dst", None, None, None),
        P("src", "dst", None),
    )
    out_specs = (
        P("src", "dst", None, None),
        P("src", "dst", None),
        P("src", "dst", None, None),
        P("src", "dst", None),
        P(("src", "dst"), None),
        P(("src", "dst")),
    )
    return jax.shard_map(
        on_device, mesh=mesh, in_specs=in_specs, out_specs=out_specs, check_vma=False
    )
```

```python
import jax
import jax.numpy as jnp
from jax import lax
from jax.experimental import pallas as pl
from jax.experimental.pallas import tpu as pltpu
from jax.sharding import PartitionSpec as P

MESH = pl.DeviceIdType.MESH
F32, BF16, I32 = jnp.float32, jnp.bfloat16, jnp.int32
ORDERS = (("z", "y", "x"), ("x", "y", "z"), ("x", "z", "y"))
SIZE = {"x": 4, "y": 8, "z": 8}
THIRDS = (0, 2, 1)
ALONG_X = (2, 1)
STEPS = 3
VMEM_LIMIT = 60 * 2**20
EDGES_1, EDGES_2, NEXT, SRC_END, DST_END = (0, 31), (0, 30), (1, 31), (1, 2), (0, 3)


def coords():
    s, d = lax.axis_index("src"), lax.axis_index("dst")
    return {
        "core": lax.rem(s, 2),
        "x": lax.rem(lax.div(s, 2), 4),
        "y": lax.div(s, 8) * 4 + lax.rem(d, 4),
        "z": lax.div(d, 4),
    }


def device_of(at):
    return (
        lax.div(at["y"], 4) * 8 + at["x"] * 2 + at["core"],
        at["z"] * 4 + lax.rem(at["y"], 4),
    )


def partner(me, axis, offset):
    return device_of({**me, axis: lax.rem(me[axis] + offset, SIZE[axis])})


def moved(offset):
    s, d = lax.axis_index("src"), lax.axis_index("dst")
    return (lax.rem(s + offset[0], 16), lax.rem(d + offset[1], 32))


def dot(a, b):
    return jnp.dot(a, b, preferred_element_type=F32)


def dot_nt(a, b):
    return lax.dot_general(a, b, (((1,), (1,)), ((), ())), preferred_element_type=F32)


def one_hot(mask):
    return jnp.where(mask, 1.0, 0.0).astype(BF16)


def split(value, axis=0):
    high = value.astype(BF16)
    low = (value - high.astype(F32)).astype(BF16)
    return jnp.concatenate([high, low], axis=axis)


def sigmoid(value):
    return 1.0 / (1.0 + jnp.exp(-value))


def eye(n):
    return lax.broadcasted_iota(I32, (n, n), 0) == lax.broadcasted_iota(I32, (n, n), 1)


def as_column(row):
    return jnp.sum(jnp.where(eye(row.shape[1]), row, 0.0), axis=1, keepdims=True)


def as_row(column):
    return jnp.sum(jnp.where(eye(column.shape[0]), column, 0.0), axis=0, keepdims=True)


def adagrad(block, state_row, grad):
    state = as_column(state_row) + jnp.sum(grad * grad, axis=1, keepdims=True) * (1.0 / 384)
    return block - 0.1 * grad / jnp.sqrt(state), as_row(state)


def positions(r, c):
    k, z, x = r & 3, (r >> 4) & 7, (r >> 8) & 3
    y = ((r >> 10) << 2) | ((r >> 2) & 3)
    at = {"x": x, "y": y, "z": z}
    first, second, third = ORDERS[c]
    return ((at[first] * SIZE[second] + at[second]) * SIZE[third] + at[third]) * 4 + k


def window_kernel(
    src_hbm, src_st_hbm, dst_hbm, dst_st_hbm, rel_hbm, rel_st_hbm, s_hbm, d_hbm, r_hbm, n_hbm, count_hbm,
    src_out, src_st_out, dst_out, dst_st_out, rel_out, rel_st_out,
    table, rel_st, s_raw, d_raw, r_raw, n_raw, r_smem, count_smem,
    idx_mine, idx, idx_sib, idx_smem, src_in, src_st_in, src_new, src_st_new, dst_cur, dst_st_cur,
    rel_vec, v_own, v_sib, half, *rest,
):
    relay_in, near_in, recv, held = rest[0], rest[1], rest[2:4], rest[4:6]
    z_relay, z_part, z_near = rest[6:9]
    (load_sem, smem_sem, idx_sem, sib_idx_sem, block_sem, state_sem, v_sem, end_sem,
     x_sem, z_sem, ring_sem) = rest[9:]
    me = coords()
    sibling = device_of({**me, "core": 1 - me["core"]})

    loads = [
        pltpu.make_async_copy(source, target, load_sem.at[i])
        for i, (source, target) in enumerate(
            [
                (r_hbm, r_smem), (count_hbm, count_smem), (rel_hbm, table),
                (s_hbm, s_raw), (d_hbm, d_raw), (r_hbm, r_raw), (n_hbm, n_raw),
                (src_hbm, src_in.at[0]), (dst_hbm, dst_cur),
                (src_st_hbm, src_st_in.at[0]), (dst_st_hbm, dst_st_cur), (rel_st_hbm, rel_st),
            ]
        )
    ]
    for load in loads:
        load.start()

    barrier = pltpu.get_barrier_semaphore()
    pl.semaphore_signal(barrier, inc=1, device_id=sibling, device_id_type=MESH)
    for ds, dd in (NEXT, EDGES_1, EDGES_2, SRC_END, DST_END):
        for offset in ((ds, dd), ((16 - ds) % 16, (32 - dd) % 32)):
            pl.semaphore_signal(barrier, inc=1, device_id=moved(offset), device_id_type=MESH)

    for axis in "xyz":

        @pl.loop(1, SIZE[axis])
        def _(o):
            pl.semaphore_signal(
                barrier, inc=1, device_id=partner(me, axis, o), device_id_type=MESH
            )

    half[...] = jnp.zeros_like(half)
    for load in loads:
        load.wait()
    block_of = lax.broadcasted_iota(I32, (1, 256), 1) >> 7
    for t in range(STEPS):
        idx_mine[t, 0:1, :] = s_raw[t]
        idx_mine[t, 1:2, :] = d_raw[t]
        idx_mine[t, 2:3, :] = r_raw[t]
        idx_mine[t, 3:4, 0:128] = n_raw[t, 0:1, :]
        idx_mine[t, 3:4, 128:256] = n_raw[t, 1:2, :]
        live = jnp.where(block_of < count_smem[0, t], 1, 0)
        idx_mine[t, 4:8, :] = jnp.broadcast_to(live, (4, 256))
    idx[0] = idx_mine[0]

    def remote(source, target, sems, to):
        return pltpu.make_async_remote_copy(
            source, target, sems.at[0], sems.at[1], device_id=to, device_id_type=MESH
        )

    def edge_copy(t, offset):
        return remote(idx_mine.at[t], idx.at[t], idx_sem.at[t], moved(offset))

    def sib_idx_copy(t):
        return remote(idx.at[t], idx_sib.at[t], sib_idx_sem.at[t], sibling)

    def v_copy(t, c):
        return remote(v_own.at[t, c], v_sib.at[t, c], v_sem.at[t, c], sibling)

    def send_v(t):
        for c in THIRDS:
            v_copy(t, c).start()

    def block_copy(t):
        return remote(src_new.at[t], src_in.at[t + 1], block_sem.at[t], moved(NEXT))

    def state_copy(t):
        return remote(src_st_new.at[t], src_st_in.at[t + 1], state_sem.at[t], moved(NEXT))

    ends = [
        remote(src_st_new.at[2], src_st_out, end_sem.at[0], moved(SRC_END)),
        remote(src_new.at[2], src_out, end_sem.at[1], moved(SRC_END)),
        remote(dst_st_cur, dst_st_out, end_sem.at[2], moved(DST_END)),
        remote(dst_cur, dst_out, end_sem.at[3], moved(DST_END)),
    ]

    def gather_relations(row_of):
        @pl.loop(0, 32)
        def _(i):
            for j in range(8):
                e = i * 8 + j
                rel_vec[pl.ds(e, 1), :] = table[pl.ds(row_of(e), 1), :]

    def add_third(t, c):
        v = jnp.concatenate(
            [v_own[t, c], v_sib[t, c]], axis=0
        )
        rhs = split(v, axis=1)
        r = jnp.concatenate([idx[t, 2:3, :], idx_sib[t, 2:3, :]], axis=1)
        at = jnp.where(((r >> 7) & 1) == me["core"], positions(r, c), -1)

        @pl.loop(0, 4)
        def _(ch):
            rows = pl.ds(pl.multiple_of(ch * 256, 256), 256)
            hot = one_hot(lax.broadcasted_iota(I32, (256, 512), 0) + ch * 256 == at)
            both = dot(hot, rhs)
            half[c, rows, :] += both[:, :128] + both[:, 128:]

    def work(t, wait_src, send_values, send_src):
        rows = idx[t]
        columns = jnp.transpose(rows.astype(F32)).astype(I32)
        s_col, d_col, n_col = columns[:, 0:1], columns[:, 1:2], columns[:, 3:4]
        live = columns[:, 4:5].astype(F32)
        lanes = lax.broadcasted_iota(I32, (256, 256), 1) & 127
        dst_blk = dst_cur[...]
        dst_two = split(dst_blk)
        dst_vec = dot(one_hot(lanes == d_col), dst_two)
        negb = dot(one_hot(lanes[:, :128] == n_col), dst_two[:128]).astype(BF16)
        s_edge = one_hot(lanes == s_col)
        subl = lax.broadcasted_iota(I32, (128, 256), 0)
        s_hot, d_hot, n_hot = (one_hot(subl == rows[i : i + 1]) for i in (0, 1, 3))
        wait_src()
        src_blk = src_in[t]
        src_vec = dot(s_edge, split(src_blk))
        rel = rel_vec[...]
        a = src_vec * rel
        ab = a.astype(BF16)
        pos = jnp.sum(a * dst_vec, axis=1, keepdims=True)
        gpos = -sigmoid(-pos) * live
        negs_part, rows_part = [], []
        for c in range(2):
            block = slice(c * 128, (c + 1) * 128)
            neg = dot_nt(ab[block], negb[block])
            gneg = sigmoid(neg) * (1.0 / 128) * live[block]
            negs_part.append(dot(gneg.astype(BF16), negb[block]))
            rows_part.append(dot(jnp.transpose(gneg).astype(BF16), ab[block]))
        gprod = gpos * dst_vec + jnp.concatenate(negs_part, axis=0)
        v = gprod * src_vec
        for c in range(3):
            v_own[t, c] = v[:, c * 128 : (c + 1) * 128]
        send_values()
        grad_src = dot(jnp.concatenate([s_hot, s_hot], axis=1), split(gprod * rel))
        block, state = adagrad(src_blk, src_st_in[t], grad_src)
        src_new[t] = block
        src_st_new[t] = state

        send_src()
        grad_dst = dot(
            jnp.concatenate([d_hot, d_hot, n_hot, n_hot], axis=1),
            jnp.concatenate([split(gpos * a), split(jnp.concatenate(rows_part, axis=0))], axis=0),
        )
        block, state = adagrad(dst_blk, dst_st_cur[...], grad_dst)
        dst_cur[...] = block
        dst_st_cur[...] = state

    def enter():
        pl.semaphore_wait(barrier, 28)

    def first_sends():
        enter()
        state_copy(0).start()
        block_copy(0).start()
        edge_copy(1, EDGES_1).start()
        edge_copy(2, EDGES_2).start()
        sib_idx_copy(0).start()
        send_v(0)

    gather_relations(lambda e: r_smem[0, 0, e])
    work(0, lambda: None, lambda: None, first_sends)

    @pl.loop(1, STEPS)
    def _(t):
        edge_copy(t, EDGES_1).wait()
        sib_idx_copy(t).start()
        load = pltpu.make_async_copy(idx.at[t], idx_smem.at[t], smem_sem)
        load.start()
        load.wait()
        gather_relations(lambda e: idx_smem[t, 2, e])

        def wait_src():
            state_copy(t - 1).wait()
            block_copy(t - 1).wait()

        def send_src():
            @pl.when(t < 2)
            def _():
                state_copy(t).start()
                block_copy(t).start()
                send_v(t)

            @pl.when(t == 2)
            def _():
                ends[0].start()
                ends[1].start()

        def send_values():
            @pl.when(t == 2)
            def _():
                send_v(t)

        work(t, wait_src, send_values, send_src)

        @pl.when(t == 2)
        def _():
            ends[2].start()
            ends[3].start()

        sib_idx_copy(t - 1).wait()
        for c in THIRDS:
            v_copy(t - 1, c).wait()
            add_third(t - 1, c)

    ahead, across, behind = (lax.rem(me["x"] + o, 4) for o in (1, 2, 3))

    def x_copy(c, k):
        lower, upper = 0, 128
        chunk, first, target, step = (
            (across, lower, relay_in.at[c, 0], 1),
            (across, upper, relay_in.at[c, 1], 3),
            (ahead, upper, near_in.at[c, 0], 1),
            (behind, lower, near_in.at[c, 1], 3),
            (ahead, lower, near_in.at[c, 2], 1),
            (behind, upper, near_in.at[c, 3], 3),
        )[k]
        source = half.at[c, pl.ds(pl.multiple_of(chunk * 256 + first, 128), 128)]
        return remote(source, target, x_sem.at[c, k], partner(me, "x", step))

    z_at = [lax.rem(me["z"] + o, 8) for o in range(8)]

    def z_rows(chunk, first, count):
        return pl.ds(pl.multiple_of(z_at[chunk] * 128 + first, count), count)

    def z_copy(k):
        chunk, first, count, target, step = (
            (3, 0, 128, z_relay.at[0], 1),
            (5, 0, 128, z_relay.at[1], 7),
            (4, 0, 64, z_part.at[0], 2),
            (4, 64, 64, z_part.at[1], 6),
            (1, 0, 128, z_near.at[0], 1),
            (7, 0, 128, z_near.at[1], 7),
            (2, 0, 128, z_near.at[2], 2),
            (6, 0, 128, z_near.at[3], 6),
        )[k]
        return remote(
            half.at[0, z_rows(chunk, first, count)], target, z_sem.at[k], partner(me, "z", step)
        )

    def ring_rows(c, p, j):
        if p == 1:
            return pl.ds(pl.multiple_of(lax.div(j, 2) * 8, 8), 8)
        count = 16 if c == 0 else 32
        return pl.ds(pl.multiple_of(j * count, count), count)

    def ring_in(c, p):
        return recv[p].at[c, 0 : SIZE[ORDERS[c][p + 1]] - 1, 0 : (8 if p else 16 if c == 0 else 32)]

    def ring_start(c, p):
        axis = ORDERS[c][p + 1]
        for o in range(1, SIZE[axis]):
            target = lax.rem(me[axis] + o, SIZE[axis])
            pltpu.make_async_remote_copy(
                held[p].at[c, ring_rows(c, p, target)],
                ring_in(c, p).at[o - 1],
                ring_sem.at[c, p, 0],
                ring_sem.at[c, p, 1],
                device_id=partner(me, axis, o),
                device_id_type=MESH,
            ).start()

    def ring_all(c, p):
        return remote(ring_in(c, p), ring_in(c, p), ring_sem.at[c, p], sibling)

    def ring_finish(c, p):
        axis = ORDERS[c][p + 1]
        ring_all(c, p).wait_recv()
        total = held[p][c, ring_rows(c, p, me[axis]), :]
        count = total.shape[0]
        for o in range(SIZE[axis] - 1):
            total = total + recv[p][c, o, 0:count]
        return total

    sib_idx_copy(2).wait()
    for c in THIRDS:
        v_copy(2, c).wait()
        add_third(2, c)
        if c == 0:
            for k in range(6):
                z_copy(k).start()
        else:
            for k in range(4):
                x_copy(c, k).start()

    def relay_x(c):
        for k, chunk, first in ((0, ahead, 0), (1, behind, 128)):
            x_copy(c, k).wait_recv()
            rows = pl.ds(pl.multiple_of(chunk * 256 + first, 128), 128)
            half[c, rows, :] += relay_in[c, k]
            x_copy(c, 4 + k).start()

    def relay_z():
        for k, chunk, first in ((0, 2, 0), (1, 6, 64)):
            z_copy(k).wait_recv()
            half[0, z_rows(chunk, 0, 128), :] += z_relay[k]
            z_copy(2 + k).wait_recv()
            half[0, z_rows(chunk, first, 64), :] += z_part[k]
            z_copy(6 + k).start()

    relay_x(2)
    relay_z()
    relay_x(1)
    own = pl.multiple_of(me["x"] * 256, 256)

    def finish_x(c):
        for k in range(2, 6):
            x_copy(c, k).wait_recv()
        held[0][c, 0:128, :] = half[c, pl.ds(own, 128), :] + near_in[c, 1] + near_in[c, 2]
        held[0][c, 128:256, :] = (
            half[c, pl.ds(pl.multiple_of(own + 128, 128), 128), :] + near_in[c, 0] + near_in[c, 3]
        )
        ring_start(c, 0)

    def finish_z():
        for k in range(4, 8):
            z_copy(k).wait_recv()
        total = half[0, z_rows(0, 0, 128), :]
        for k in range(4):
            total = total + z_near[k]
        held[0][0, 0:128, :] = total
        ring_start(0, 0)

    finish_x(2)
    finish_z()
    finish_x(1)
    for c in (2, 0, 1):
        total = ring_finish(c, 0)
        held[1][c, 0 : total.shape[0], :] = total
        ring_start(c, 1)
    last = {}
    for c in (2, 0, 1):
        total = ring_finish(c, 1)
        odd = lax.rem(me[ORDERS[c][2]], 2)
        last[c] = jnp.where(odd == 0, total[0:4], total[4:8])
    grad = jnp.concatenate([last[0], last[1], last[2]], axis=1)
    owner = lax.axis_index("src") * 32 + lax.axis_index("dst")
    near = table[pl.ds(pl.multiple_of(lax.div(owner, 2) * 8, 8), 8), :]
    own_rel = jnp.where(lax.rem(owner, 2) == 0, near[0:4], near[4:8])
    state = as_column(rel_st[...]) + jnp.sum(grad * grad, axis=1, keepdims=True) * (1.0 / 384)
    rel_st_out[...] = as_row(state)
    rel_out[...] = own_rel - 0.1 * grad / jnp.sqrt(state)
    for k in range(8):
        z_copy(k).wait_send()
    for c in ALONG_X:
        for k in range(6):
            x_copy(c, k).wait_send()
    for c in THIRDS:
        for p in range(2):
            ring_all(c, p).wait_send()
    for copy in ends:
        copy.wait()


def store_kernel(*refs):
    sources, targets, held, sems = refs[:6], refs[6:12], refs[12:18], refs[18]
    loads = [pltpu.make_async_copy(sources[i], held[i], sems.at[0, i]) for i in range(6)]
    stores = [pltpu.make_async_copy(held[i], targets[i], sems.at[1, i]) for i in range(6)]
    for load in loads:
        load.start()
    for load, store in zip(loads, stores):
        load.wait()
        store.start()
    for store in stores:
        store.wait()


def on_device(
    source_embedding_table,
    source_adagrad_state,
    destination_embedding_table,
    destination_adagrad_state,
    relations,
    rel_state,
    source_edge_rows,
    destination_edge_rows,
    edge_relation_index,
    negative_block_rows,
    bucket_block_counts,
):
    vmem, hbm = pl.BlockSpec(memory_space=pltpu.VMEM), pl.BlockSpec(memory_space=pl.ANY)
    dma = pltpu.SemaphoreType.DMA
    scratch = [
        pltpu.VMEM((2048, 384), F32),
        pltpu.VMEM((1, 4), F32),
        pltpu.VMEM((3, 1, 256), I32),
        pltpu.VMEM((3, 1, 256), I32),
        pltpu.VMEM((3, 1, 256), I32),
        pltpu.VMEM((3, 2, 128), I32),
        pltpu.SMEM((3, 1, 256), I32),
        pltpu.SMEM((1, 3), I32),
        pltpu.VMEM((3, 8, 256), I32),
        pltpu.VMEM((3, 8, 256), I32),
        pltpu.VMEM((3, 8, 256), I32),
        pltpu.SMEM((3, 8, 256), I32),
        pltpu.VMEM((3, 128, 384), F32),
        pltpu.VMEM((3, 1, 128), F32),
        pltpu.VMEM((3, 128, 384), F32),
        pltpu.VMEM((3, 1, 128), F32),
        pltpu.VMEM((128, 384), F32),
        pltpu.VMEM((1, 128), F32),
        pltpu.VMEM((256, 384), F32),
        pltpu.VMEM((3, 3, 256, 128), F32),
        pltpu.VMEM((3, 3, 256, 128), F32),
        pltpu.VMEM((3, 1024, 128), F32),
    ]
    scratch += [
        pltpu.VMEM((3, 2, 128, 128), F32),
        pltpu.VMEM((3, 4, 128, 128), F32),
        pltpu.VMEM((3, 7, 32, 128), F32),
        pltpu.VMEM((3, 7, 8, 128), F32),
        pltpu.VMEM((3, 256, 128), F32),
        pltpu.VMEM((3, 32, 128), F32),
        pltpu.VMEM((2, 128, 128), F32),
        pltpu.VMEM((2, 64, 128), F32),
        pltpu.VMEM((4, 128, 128), F32),
    ]
    scratch += [dma((12,)), dma, dma((3, 2)), dma((3, 2)), dma((2, 2)), dma((2, 2)), dma((3, 3, 2)), dma((4, 2))]
    scratch += [dma((3, 6, 2)), dma((8, 2)), dma((3, 2, 2))]
    block = jax.ShapeDtypeStruct((128, 384), F32)
    row = jax.ShapeDtypeStruct((1, 128), F32)
    results = (block, row, block, row)
    results += (jax.ShapeDtypeStruct((4, 384), F32), jax.ShapeDtypeStruct((1, 4), F32))
    outs = pl.pallas_call(
        window_kernel,
        out_shape=results,
        in_specs=[hbm] * 11,
        out_specs=(hbm,) * 4 + (vmem,) * 2,
        scratch_shapes=scratch,
        compiler_params=pltpu.CompilerParams(
            collective_id=0, has_side_effects=True, vmem_limit_bytes=VMEM_LIMIT
        ),
    )(
        source_embedding_table[0, 0],
        source_adagrad_state[0],
        destination_embedding_table[0, 0],
        destination_adagrad_state[0],
        relations,
        rel_state[None],
        source_edge_rows.reshape(STEPS, 1, 256),
        destination_edge_rows.reshape(STEPS, 1, 256),
        edge_relation_index.reshape(STEPS, 1, 256),
        negative_block_rows[0, 0],
        bucket_block_counts[0],
    )
    src_out, src_st, dst_out, dst_st, rel_out, rel_st = pl.pallas_call(
        store_kernel,
        out_shape=results,
        in_specs=[hbm] * 6,
        out_specs=(hbm,) * 6,
        scratch_shapes=[pltpu.VMEM(r.shape, F32) for r in results] + [dma((2, 6))],
        compiler_params=pltpu.CompilerParams(vmem_limit_bytes=VMEM_LIMIT),
    )(*outs)
    return (
        src_out[None, None],
        src_st[None],
        dst_out[None, None],
        dst_st[None],
        rel_out,
        rel_st[0],
    )


def solution(mesh):
    in_specs = (
        P("src", "dst", None, None),
        P("src", "dst", None),
        P("src", "dst", None, None),
        P("src", "dst", None),
        P(),
        P(("src", "dst")),
        P("src", "dst", None, None),
        P("src", "dst", None, None),
        P("src", "dst", None, None),
        P("src", "dst", None, None, None),
        P("src", "dst", None),
    )
    out_specs = (
        P("src", "dst", None, None),
        P("src", "dst", None),
        P("src", "dst", None, None),
        P("src", "dst", None),
        P(("src", "dst"), None),
        P(("src", "dst")),
    )
    return jax.shard_map(
        on_device, mesh=mesh, in_specs=in_specs, out_specs=out_specs, check_vma=False
    )
```

```python
import jax
import jax.numpy as jnp
from jax import lax
from jax.experimental import pallas as pl
from jax.experimental.pallas import tpu as pltpu
from jax.sharding import PartitionSpec as P

MESH = pl.DeviceIdType.MESH
F32, BF16, I32 = jnp.float32, jnp.bfloat16, jnp.int32
ORDERS = (("z", "x", "y"), ("x", "z", "y"), ("x", "z", "y"))
SIZE = {"x": 4, "y": 8, "z": 8}
THIRDS = (0, 2, 1)
ALONG_X = (2, 1)
STEPS = 3
VMEM_LIMIT = 60 * 2**20
EDGES_1, EDGES_2, NEXT, SRC_END, DST_END = (0, 31), (0, 30), (1, 31), (1, 2), (0, 3)


def coords():
    s, d = lax.axis_index("src"), lax.axis_index("dst")
    return {
        "core": lax.rem(s, 2),
        "x": lax.rem(lax.div(s, 2), 4),
        "y": lax.div(s, 8) * 4 + lax.rem(d, 4),
        "z": lax.div(d, 4),
    }


def device_of(at):
    return (
        lax.div(at["y"], 4) * 8 + at["x"] * 2 + at["core"],
        at["z"] * 4 + lax.rem(at["y"], 4),
    )


def partner(me, axis, offset):
    return device_of({**me, axis: lax.rem(me[axis] + offset, SIZE[axis])})


def moved(offset):
    s, d = lax.axis_index("src"), lax.axis_index("dst")
    return (lax.rem(s + offset[0], 16), lax.rem(d + offset[1], 32))


def dot(a, b):
    return jnp.dot(a, b, preferred_element_type=F32)


def dot_nt(a, b):
    return lax.dot_general(a, b, (((1,), (1,)), ((), ())), preferred_element_type=F32)


def one_hot(mask):
    return jnp.where(mask, 1.0, 0.0).astype(BF16)


def split(value, axis=0):
    high = value.astype(BF16)
    low = (value - high.astype(F32)).astype(BF16)
    return jnp.concatenate([high, low], axis=axis)


def sigmoid(value):
    return 1.0 / (1.0 + jnp.exp(-value))


def eye(n):
    return lax.broadcasted_iota(I32, (n, n), 0) == lax.broadcasted_iota(I32, (n, n), 1)


def as_column(row):
    return jnp.sum(jnp.where(eye(row.shape[1]), row, 0.0), axis=1, keepdims=True)


def as_row(column):
    return jnp.sum(jnp.where(eye(column.shape[0]), column, 0.0), axis=0, keepdims=True)


def adagrad(block, state_row, grad):
    state = as_column(state_row) + jnp.sum(grad * grad, axis=1, keepdims=True) * (1.0 / 384)
    return block - 0.1 * grad / jnp.sqrt(state), as_row(state)


def positions(r, c):
    k, z, x = r & 3, (r >> 4) & 7, (r >> 8) & 3
    y = ((r >> 10) << 2) | ((r >> 2) & 3)
    at = {"x": x, "y": y, "z": z}
    first, second, third = ORDERS[c]
    return ((at[first] * SIZE[second] + at[second]) * SIZE[third] + at[third]) * 4 + k


def window_kernel(
    src_hbm, src_st_hbm, dst_hbm, dst_st_hbm, rel_hbm, rel_st_hbm, s_hbm, d_hbm, r_hbm, n_hbm, count_hbm,
    src_out, src_st_out, dst_out, dst_st_out, rel_out, rel_st_out,
    table, rel_st, s_raw, d_raw, r_raw, n_raw, r_smem, count_smem,
    idx_mine, idx, idx_sib, idx_smem, src_in, src_st_in, src_new, src_st_new, dst_cur, dst_st_cur,
    rel_vec, v_own, v_sib, half, *rest,
):
    relay_in, near_in, recv, held = rest[0], rest[1], rest[2:4], rest[4:6]
    z_relay, z_part, z_near = rest[6:9]
    (load_sem, smem_sem, idx_sem, sib_idx_sem, block_sem, state_sem, v_sem, end_sem,
     x_sem, z_sem, ring_sem) = rest[9:]
    me = coords()
    sibling = device_of({**me, "core": 1 - me["core"]})

    loads = [
        pltpu.make_async_copy(source, target, load_sem.at[i])
        for i, (source, target) in enumerate(
            [
                (r_hbm, r_smem), (count_hbm, count_smem), (rel_hbm, table),
                (s_hbm, s_raw), (d_hbm, d_raw), (r_hbm, r_raw), (n_hbm, n_raw),
                (src_hbm, src_in.at[0]), (dst_hbm, dst_cur),
                (src_st_hbm, src_st_in.at[0]), (dst_st_hbm, dst_st_cur), (rel_st_hbm, rel_st),
            ]
        )
    ]
    for load in loads:
        load.start()

    barrier = pltpu.get_barrier_semaphore()
    pl.semaphore_signal(barrier, inc=1, device_id=sibling, device_id_type=MESH)
    for ds, dd in (NEXT, EDGES_1, EDGES_2, SRC_END, DST_END):
        for offset in ((ds, dd), ((16 - ds) % 16, (32 - dd) % 32)):
            pl.semaphore_signal(barrier, inc=1, device_id=moved(offset), device_id_type=MESH)

    for axis in "xyz":

        @pl.loop(1, SIZE[axis])
        def _(o):
            pl.semaphore_signal(
                barrier, inc=1, device_id=partner(me, axis, o), device_id_type=MESH
            )

    for load in loads:
        load.wait()
    block_of = lax.broadcasted_iota(I32, (1, 256), 1) >> 7

    def pack(t):
        idx_mine[t, 0:1, :] = s_raw[t]
        idx_mine[t, 1:2, :] = d_raw[t]
        idx_mine[t, 2:3, :] = r_raw[t]
        idx_mine[t, 3:4, 0:128] = n_raw[t, 0:1, :]
        idx_mine[t, 3:4, 128:256] = n_raw[t, 1:2, :]
        live = jnp.where(block_of < count_smem[0, t], 1, 0)
        idx_mine[t, 4:8, :] = jnp.broadcast_to(live, (4, 256))

    pack(0)
    idx[0] = idx_mine[0]

    def remote(source, target, sems, to):
        return pltpu.make_async_remote_copy(
            source, target, sems.at[0], sems.at[1], device_id=to, device_id_type=MESH
        )

    def edge_copy(t, offset):
        return remote(idx_mine.at[t], idx.at[t], idx_sem.at[t], moved(offset))

    def sib_idx_copy(t):
        return remote(idx.at[t], idx_sib.at[t], sib_idx_sem.at[t], sibling)

    def v_copy(t, c):
        return remote(v_own.at[t, c], v_sib.at[t, c], v_sem.at[t, c], sibling)

    def send_v(t):
        for c in THIRDS:
            v_copy(t, c).start()

    def block_copy(t):
        return remote(src_new.at[t], src_in.at[t + 1], block_sem.at[t], moved(NEXT))

    def state_copy(t):
        return remote(src_st_new.at[t], src_st_in.at[t + 1], state_sem.at[t], moved(NEXT))

    ends = [
        remote(src_st_new.at[2], src_st_out, end_sem.at[0], moved(SRC_END)),
        remote(src_new.at[2], src_out, end_sem.at[1], moved(SRC_END)),
        remote(dst_st_cur, dst_st_out, end_sem.at[2], moved(DST_END)),
        remote(dst_cur, dst_out, end_sem.at[3], moved(DST_END)),
    ]

    def gather_relations(row_of):
        @pl.loop(0, 32)
        def _(i):
            for j in range(8):
                e = i * 8 + j
                rel_vec[pl.ds(e, 1), :] = table[pl.ds(row_of(e), 1), :]

    def add_third(t, c):
        v = jnp.concatenate(
            [v_own[t, c], v_sib[t, c]], axis=0
        )
        rhs = split(v, axis=1)
        r = jnp.concatenate([idx[t, 2:3, :], idx_sib[t, 2:3, :]], axis=1)
        at = jnp.where(((r >> 7) & 1) == me["core"], positions(r, c), -1)

        @pl.loop(0, 4)
        def _(ch):
            rows = pl.ds(pl.multiple_of(ch * 256, 256), 256)
            hot = one_hot(lax.broadcasted_iota(I32, (256, 512), 0) + ch * 256 == at)
            both = dot(hot, rhs)
            half[c, rows, :] += both[:, :128] + both[:, 128:]

    def work(t, send_values, send_src):
        rows = idx[t]
        columns = jnp.transpose(rows.astype(F32)).astype(I32)
        s_col, d_col, n_col = columns[:, 0:1], columns[:, 1:2], columns[:, 3:4]
        live = columns[:, 4:5].astype(F32)
        lanes = lax.broadcasted_iota(I32, (256, 256), 1) & 127
        src_blk, dst_blk = src_in[t], dst_cur[...]
        dst_two = split(dst_blk)
        src_vec = dot(one_hot(lanes == s_col), split(src_blk))
        dst_vec = dot(one_hot(lanes == d_col), dst_two)
        negb = dot(one_hot(lanes[:, :128] == n_col), dst_two[:128]).astype(BF16)
        rel = rel_vec[...]
        a = src_vec * rel
        ab = a.astype(BF16)
        pos = jnp.sum(a * dst_vec, axis=1, keepdims=True)
        gpos = -sigmoid(-pos) * live
        negs_part, rows_part = [], []
        for c in range(2):
            block = slice(c * 128, (c + 1) * 128)
            neg = dot_nt(ab[block], negb[block])
            gneg = sigmoid(neg) * (1.0 / 128) * live[block]
            negs_part.append(dot(gneg.astype(BF16), negb[block]))
            rows_part.append(dot(jnp.transpose(gneg).astype(BF16), ab[block]))
        gprod = gpos * dst_vec + jnp.concatenate(negs_part, axis=0)
        v = gprod * src_vec
        for c in range(3):
            v_own[t, c] = v[:, c * 128 : (c + 1) * 128]
        send_values()
        subl = lax.broadcasted_iota(I32, (128, 256), 0)
        s_hot = one_hot(subl == rows[0:1])
        grad_src = dot(jnp.concatenate([s_hot, s_hot], axis=1), split(gprod * rel))
        block, state = adagrad(src_blk, src_st_in[t], grad_src)
        src_new[t] = block
        src_st_new[t] = state

        send_src()
        d_hot = one_hot(subl == rows[1:2])
        n_hot = one_hot(subl == rows[3:4])
        grad_dst = dot(
            jnp.concatenate([d_hot, d_hot, n_hot, n_hot], axis=1),
            jnp.concatenate([split(gpos * a), split(jnp.concatenate(rows_part, axis=0))], axis=0),
        )
        block, state = adagrad(dst_blk, dst_st_cur[...], grad_dst)
        dst_cur[...] = block
        dst_st_cur[...] = state

    def enter():
        pl.semaphore_wait(barrier, 28)

    def first_sends():
        enter()
        state_copy(0).start()
        block_copy(0).start()
        pack(1)
        pack(2)
        edge_copy(1, EDGES_1).start()
        edge_copy(2, EDGES_2).start()
        sib_idx_copy(0).start()
        send_v(0)
        half[...] = jnp.zeros_like(half)

    gather_relations(lambda e: r_smem[0, 0, e])
    work(0, lambda: None, first_sends)

    @pl.loop(1, STEPS)
    def _(t):
        edge_copy(t, EDGES_1).wait()
        sib_idx_copy(t).start()
        load = pltpu.make_async_copy(idx.at[t], idx_smem.at[t], smem_sem)
        load.start()
        load.wait()
        gather_relations(lambda e: idx_smem[t, 2, e])
        state_copy(t - 1).wait()
        block_copy(t - 1).wait()

        def send_src():
            @pl.when(t < 2)
            def _():
                state_copy(t).start()
                block_copy(t).start()

            @pl.when(t == 2)
            def _():
                ends[0].start()
                ends[1].start()

        work(t, lambda: send_v(t), send_src)

        @pl.when(t == 2)
        def _():
            ends[2].start()
            ends[3].start()

        sib_idx_copy(t - 1).wait()
        for c in THIRDS:
            v_copy(t - 1, c).wait()
            add_third(t - 1, c)

    ahead, across, behind = (lax.rem(me["x"] + o, 4) for o in (1, 2, 3))

    def x_copy(c, k):
        lower, upper = 0, 128
        chunk, first, target, step = (
            (across, lower, relay_in.at[c, 0], 1),
            (across, upper, relay_in.at[c, 1], 3),
            (ahead, upper, near_in.at[c, 0], 1),
            (behind, lower, near_in.at[c, 1], 3),
            (ahead, lower, near_in.at[c, 2], 1),
            (behind, upper, near_in.at[c, 3], 3),
        )[k]
        source = half.at[c, pl.ds(pl.multiple_of(chunk * 256 + first, 128), 128)]
        return remote(source, target, x_sem.at[c, k], partner(me, "x", step))

    z_at = [lax.rem(me["z"] + o, 8) for o in range(8)]

    def z_rows(chunk, first, count):
        return pl.ds(pl.multiple_of(z_at[chunk] * 128 + first, count), count)

    def z_copy(k):
        chunk, first, count, target, step = (
            (3, 0, 128, z_relay.at[0], 1),
            (5, 0, 128, z_relay.at[1], 7),
            (4, 0, 64, z_part.at[0], 2),
            (4, 64, 64, z_part.at[1], 6),
            (1, 0, 128, z_near.at[0], 1),
            (7, 0, 128, z_near.at[1], 7),
            (2, 0, 128, z_near.at[2], 2),
            (6, 0, 128, z_near.at[3], 6),
        )[k]
        return remote(
            half.at[0, z_rows(chunk, first, count)], target, z_sem.at[k], partner(me, "z", step)
        )

    def ring_rows(c, p, j):
        if p == 1:
            return pl.ds(pl.multiple_of(lax.div(j, 2) * 8, 8), 8)
        return pl.ds(pl.multiple_of(j * ring_count(c, p), ring_count(c, p)), ring_count(c, p))

    def ring_count(c, p):
        return 8 if p else 1024 // SIZE[ORDERS[c][0]] // SIZE[ORDERS[c][1]]

    def ring_in(c, p):
        return recv[p].at[c, 0 : SIZE[ORDERS[c][p + 1]] - 1, 0 : ring_count(c, p)]

    def ring_start(c, p):
        axis = ORDERS[c][p + 1]
        for o in range(1, SIZE[axis]):
            target = lax.rem(me[axis] + o, SIZE[axis])
            pltpu.make_async_remote_copy(
                held[p].at[c, ring_rows(c, p, target)],
                ring_in(c, p).at[o - 1],
                ring_sem.at[c, p, 0],
                ring_sem.at[c, p, 1],
                device_id=partner(me, axis, o),
                device_id_type=MESH,
            ).start()

    def ring_all(c, p):
        return remote(ring_in(c, p), ring_in(c, p), ring_sem.at[c, p], sibling)

    def ring_finish(c, p):
        axis = ORDERS[c][p + 1]
        ring_all(c, p).wait_recv()
        total = held[p][c, ring_rows(c, p, me[axis]), :]
        count = total.shape[0]
        for o in range(SIZE[axis] - 1):
            total = total + recv[p][c, o, 0:count]
        return total

    sib_idx_copy(2).wait()
    for c in THIRDS:
        v_copy(2, c).wait()
        add_third(2, c)
        if c == 0:
            for k in range(6):
                z_copy(k).start()
        else:
            for k in range(4):
                x_copy(c, k).start()

    def relay_x(c):
        for k, chunk, first in ((0, ahead, 0), (1, behind, 128)):
            x_copy(c, k).wait_recv()
            rows = pl.ds(pl.multiple_of(chunk * 256 + first, 128), 128)
            half[c, rows, :] += relay_in[c, k]
            x_copy(c, 4 + k).start()

    def relay_z():
        for k, chunk, first in ((0, 2, 0), (1, 6, 64)):
            z_copy(k).wait_recv()
            half[0, z_rows(chunk, 0, 128), :] += z_relay[k]
            z_copy(2 + k).wait_recv()
            half[0, z_rows(chunk, first, 64), :] += z_part[k]
            z_copy(6 + k).start()

    relay_x(2)
    relay_z()
    relay_x(1)
    own = pl.multiple_of(me["x"] * 256, 256)

    def finish_x(c):
        for k in range(2, 6):
            x_copy(c, k).wait_recv()
        held[0][c, 0:128, :] = half[c, pl.ds(own, 128), :] + near_in[c, 1] + near_in[c, 2]
        held[0][c, 128:256, :] = (
            half[c, pl.ds(pl.multiple_of(own + 128, 128), 128), :] + near_in[c, 0] + near_in[c, 3]
        )
        ring_start(c, 0)

    def finish_z():
        for k in range(4, 8):
            z_copy(k).wait_recv()
        total = half[0, z_rows(0, 0, 128), :]
        for k in range(4):
            total = total + z_near[k]
        held[0][0, 0:128, :] = total
        ring_start(0, 0)

    finish_x(2)
    finish_z()
    finish_x(1)
    for c in (2, 0, 1):
        total = ring_finish(c, 0)
        held[1][c, 0 : total.shape[0], :] = total
        ring_start(c, 1)
    last = {}
    for c in (2, 0, 1):
        total = ring_finish(c, 1)
        odd = lax.rem(me[ORDERS[c][2]], 2)
        last[c] = jnp.where(odd == 0, total[0:4], total[4:8])
    grad = jnp.concatenate([last[0], last[1], last[2]], axis=1)
    owner = lax.axis_index("src") * 32 + lax.axis_index("dst")
    near = table[pl.ds(pl.multiple_of(lax.div(owner, 2) * 8, 8), 8), :]
    own_rel = jnp.where(lax.rem(owner, 2) == 0, near[0:4], near[4:8])
    state = as_column(rel_st[...]) + jnp.sum(grad * grad, axis=1, keepdims=True) * (1.0 / 384)
    rel_st_out[...] = as_row(state)
    rel_out[...] = own_rel - 0.1 * grad / jnp.sqrt(state)
    for k in range(8):
        z_copy(k).wait_send()
    for c in ALONG_X:
        for k in range(6):
            x_copy(c, k).wait_send()
    for c in THIRDS:
        for p in range(2):
            ring_all(c, p).wait_send()
    for copy in ends:
        copy.wait()


def store_kernel(*refs):
    sources, targets, held, sems = refs[:6], refs[6:12], refs[12:18], refs[18]
    parts = [(i, slice(j * 32, j * 32 + 32)) for j in range(4) for i in (0, 2)]
    parts += [(i, slice(None)) for i in (1, 3, 4, 5)]
    loads = [
        pltpu.make_async_copy(sources[i].at[rows], held[i].at[rows], sems.at[0, n])
        for n, (i, rows) in enumerate(parts)
    ]
    stores = [
        pltpu.make_async_copy(held[i].at[rows], targets[i].at[rows], sems.at[1, n])
        for n, (i, rows) in enumerate(parts)
    ]
    for load in loads:
        load.start()
    for load, store in zip(loads, stores):
        load.wait()
        store.start()
    for store in stores:
        store.wait()


def on_device(
    source_embedding_table,
    source_adagrad_state,
    destination_embedding_table,
    destination_adagrad_state,
    relations,
    rel_state,
    source_edge_rows,
    destination_edge_rows,
    edge_relation_index,
    negative_block_rows,
    bucket_block_counts,
):
    vmem, hbm = pl.BlockSpec(memory_space=pltpu.VMEM), pl.BlockSpec(memory_space=pl.ANY)
    dma = pltpu.SemaphoreType.DMA
    scratch = [
        pltpu.VMEM((2048, 384), F32),
        pltpu.VMEM((1, 4), F32),
        pltpu.VMEM((3, 1, 256), I32),
        pltpu.VMEM((3, 1, 256), I32),
        pltpu.VMEM((3, 1, 256), I32),
        pltpu.VMEM((3, 2, 128), I32),
        pltpu.SMEM((3, 1, 256), I32),
        pltpu.SMEM((1, 3), I32),
        pltpu.VMEM((3, 8, 256), I32),
        pltpu.VMEM((3, 8, 256), I32),
        pltpu.VMEM((3, 8, 256), I32),
        pltpu.SMEM((3, 8, 256), I32),
        pltpu.VMEM((3, 128, 384), F32),
        pltpu.VMEM((3, 1, 128), F32),
        pltpu.VMEM((3, 128, 384), F32),
        pltpu.VMEM((3, 1, 128), F32),
        pltpu.VMEM((128, 384), F32),
        pltpu.VMEM((1, 128), F32),
        pltpu.VMEM((256, 384), F32),
        pltpu.VMEM((3, 3, 256, 128), F32),
        pltpu.VMEM((3, 3, 256, 128), F32),
        pltpu.VMEM((3, 1024, 128), F32),
    ]
    scratch += [
        pltpu.VMEM((3, 2, 128, 128), F32),
        pltpu.VMEM((3, 4, 128, 128), F32),
        pltpu.VMEM((3, 7, 32, 128), F32),
        pltpu.VMEM((3, 7, 8, 128), F32),
        pltpu.VMEM((3, 256, 128), F32),
        pltpu.VMEM((3, 32, 128), F32),
        pltpu.VMEM((2, 128, 128), F32),
        pltpu.VMEM((2, 64, 128), F32),
        pltpu.VMEM((4, 128, 128), F32),
    ]
    scratch += [dma((12,)), dma, dma((3, 2)), dma((3, 2)), dma((2, 2)), dma((2, 2)), dma((3, 3, 2)), dma((4, 2))]
    scratch += [dma((3, 6, 2)), dma((8, 2)), dma((3, 2, 2))]
    block = jax.ShapeDtypeStruct((128, 384), F32)
    row = jax.ShapeDtypeStruct((1, 128), F32)
    results = (block, row, block, row)
    results += (jax.ShapeDtypeStruct((4, 384), F32), jax.ShapeDtypeStruct((1, 4), F32))
    outs = pl.pallas_call(
        window_kernel,
        out_shape=results,
        in_specs=[hbm] * 11,
        out_specs=(hbm,) * 4 + (vmem,) * 2,
        scratch_shapes=scratch,
        compiler_params=pltpu.CompilerParams(
            collective_id=0, has_side_effects=True, vmem_limit_bytes=VMEM_LIMIT
        ),
    )(
        source_embedding_table[0, 0],
        source_adagrad_state[0],
        destination_embedding_table[0, 0],
        destination_adagrad_state[0],
        relations,
        rel_state[None],
        source_edge_rows.reshape(STEPS, 1, 256),
        destination_edge_rows.reshape(STEPS, 1, 256),
        edge_relation_index.reshape(STEPS, 1, 256),
        negative_block_rows[0, 0],
        bucket_block_counts[0],
    )
    src_out, src_st, dst_out, dst_st, rel_out, rel_st = pl.pallas_call(
        store_kernel,
        out_shape=results,
        in_specs=[hbm] * 6,
        out_specs=(hbm,) * 6,
        scratch_shapes=[pltpu.VMEM(r.shape, F32) for r in results] + [dma((2, 12))],
        compiler_params=pltpu.CompilerParams(vmem_limit_bytes=VMEM_LIMIT),
    )(*outs)
    return (
        src_out[None, None],
        src_st[None],
        dst_out[None, None],
        dst_st[None],
        rel_out,
        rel_st[0],
    )


def solution(mesh):
    in_specs = (
        P("src", "dst", None, None),
        P("src", "dst", None),
        P("src", "dst", None, None),
        P("src", "dst", None),
        P(),
        P(("src", "dst")),
        P("src", "dst", None, None),
        P("src", "dst", None, None),
        P("src", "dst", None, None),
        P("src", "dst", None, None, None),
        P("src", "dst", None),
    )
    out_specs = (
        P("src", "dst", None, None),
        P("src", "dst", None),
        P("src", "dst", None, None),
        P("src", "dst", None),
        P(("src", "dst"), None),
        P(("src", "dst")),
    )
    return jax.shard_map(
        on_device, mesh=mesh, in_specs=in_specs, out_specs=out_specs, check_vma=False
    )
```

```python
import jax
import jax.numpy as jnp
from jax import lax
from jax.experimental import pallas as pl
from jax.experimental.pallas import tpu as pltpu
from jax.sharding import PartitionSpec as P

MESH = pl.DeviceIdType.MESH
F32, BF16, I32 = jnp.float32, jnp.bfloat16, jnp.int32
ORDERS = (("z", "x", "y"), ("x", "z", "y"), ("x", "z", "y"))
SIZE = {"x": 4, "y": 8, "z": 8}
THIRDS = (0, 2, 1)
ALONG_X = (2, 1)
STEPS = 3
VMEM_LIMIT = 60 * 2**20
EDGES_1, EDGES_2, NEXT, SRC_END, DST_END = (0, 31), (0, 30), (1, 31), (1, 2), (0, 3)


def coords():
    s, d = lax.axis_index("src"), lax.axis_index("dst")
    return {
        "core": lax.rem(s, 2),
        "x": lax.rem(lax.div(s, 2), 4),
        "y": lax.div(s, 8) * 4 + lax.rem(d, 4),
        "z": lax.div(d, 4),
    }


def device_of(at):
    return (
        lax.div(at["y"], 4) * 8 + at["x"] * 2 + at["core"],
        at["z"] * 4 + lax.rem(at["y"], 4),
    )


def partner(me, axis, offset):
    return device_of({**me, axis: lax.rem(me[axis] + offset, SIZE[axis])})


def moved(offset):
    s, d = lax.axis_index("src"), lax.axis_index("dst")
    return (lax.rem(s + offset[0], 16), lax.rem(d + offset[1], 32))


def dot(a, b):
    return jnp.dot(a, b, preferred_element_type=F32)


def dot_nt(a, b):
    return lax.dot_general(a, b, (((1,), (1,)), ((), ())), preferred_element_type=F32)


def one_hot(mask):
    return jnp.where(mask, 1.0, 0.0).astype(BF16)


def split(value, axis=0):
    high = value.astype(BF16)
    low = (value - high.astype(F32)).astype(BF16)
    return jnp.concatenate([high, low], axis=axis)


def sigmoid(value):
    return 1.0 / (1.0 + jnp.exp(-value))


def eye(n):
    return lax.broadcasted_iota(I32, (n, n), 0) == lax.broadcasted_iota(I32, (n, n), 1)


def as_column(row):
    return jnp.sum(jnp.where(eye(row.shape[1]), row, 0.0), axis=1, keepdims=True)


def as_row(column):
    return jnp.sum(jnp.where(eye(column.shape[0]), column, 0.0), axis=0, keepdims=True)


def adagrad(block, state_row, grad):
    state = as_column(state_row) + jnp.sum(grad * grad, axis=1, keepdims=True) * (1.0 / 384)
    return block - 0.1 * grad / jnp.sqrt(state), as_row(state)


def positions(r, c):
    k, z, x = r & 3, (r >> 4) & 7, (r >> 8) & 3
    y = ((r >> 10) << 2) | ((r >> 2) & 3)
    at = {"x": x, "y": y, "z": z}
    first, second, third = ORDERS[c]
    return ((at[first] * SIZE[second] + at[second]) * SIZE[third] + at[third]) * 4 + k


def window_kernel(
    src_hbm, src_st_hbm, dst_hbm, dst_st_hbm, rel_hbm, rel_st_hbm, s_hbm, d_hbm, r_hbm, n_hbm, count_hbm,
    src_out, src_st_out, dst_out, dst_st_out, rel_out, rel_st_out,
    table, rel_st, s_raw, d_raw, r_raw, n_raw, r_smem, count_smem,
    idx_mine, idx, idx_sib, idx_smem, src_in, src_st_in, src_new, src_st_new, dst_cur, dst_st_cur,
    rel_vec, v_own, v_sib, half, *rest,
):
    relay_in, near_in, recv, held = rest[0], rest[1], rest[2:4], rest[4:6]
    z_relay, z_part, z_near = rest[6:9]
    (load_sem, smem_sem, idx_sem, sib_idx_sem, block_sem, state_sem, v_sem, end_sem,
     x_sem, z_sem, ring_sem) = rest[9:]
    me = coords()
    sibling = device_of({**me, "core": 1 - me["core"]})

    loads = [
        pltpu.make_async_copy(source, target, load_sem.at[i])
        for i, (source, target) in enumerate(
            [
                (r_hbm, r_smem), (count_hbm, count_smem), (rel_hbm, table),
                (s_hbm, s_raw), (d_hbm, d_raw), (r_hbm, r_raw), (n_hbm, n_raw),
                (src_hbm, src_in.at[0]), (dst_hbm, dst_cur),
                (src_st_hbm, src_st_in.at[0]), (dst_st_hbm, dst_st_cur), (rel_st_hbm, rel_st),
            ]
        )
    ]
    for load in loads:
        load.start()

    barrier = pltpu.get_barrier_semaphore()
    pl.semaphore_signal(barrier, inc=1, device_id=sibling, device_id_type=MESH)
    for ds, dd in (NEXT, EDGES_1, EDGES_2, SRC_END, DST_END):
        for offset in ((ds, dd), ((16 - ds) % 16, (32 - dd) % 32)):
            pl.semaphore_signal(barrier, inc=1, device_id=moved(offset), device_id_type=MESH)

    for axis in "xyz":

        @pl.loop(1, SIZE[axis])
        def _(o):
            pl.semaphore_signal(
                barrier, inc=1, device_id=partner(me, axis, o), device_id_type=MESH
            )

    for load in loads:
        load.wait()
    block_of = lax.broadcasted_iota(I32, (1, 256), 1) >> 7

    def pack(t):
        idx_mine[t, 0:1, :] = s_raw[t]
        idx_mine[t, 1:2, :] = d_raw[t]
        idx_mine[t, 2:3, :] = r_raw[t]
        idx_mine[t, 3:4, 0:128] = n_raw[t, 0:1, :]
        idx_mine[t, 3:4, 128:256] = n_raw[t, 1:2, :]
        live = jnp.where(block_of < count_smem[0, t], 1, 0)
        idx_mine[t, 4:8, :] = jnp.broadcast_to(live, (4, 256))

    pack(0)
    idx[0] = idx_mine[0]

    def remote(source, target, sems, to):
        return pltpu.make_async_remote_copy(
            source, target, sems.at[0], sems.at[1], device_id=to, device_id_type=MESH
        )

    def edge_copy(t, offset):
        return remote(idx_mine.at[t], idx.at[t], idx_sem.at[t], moved(offset))

    def sib_idx_copy(t):
        return remote(idx.at[t], idx_sib.at[t], sib_idx_sem.at[t], sibling)

    def v_copy(t, c):
        return remote(v_own.at[t, c], v_sib.at[t, c], v_sem.at[t, c], sibling)

    def send_v(t):
        for c in THIRDS:
            v_copy(t, c).start()

    def block_copy(t):
        return remote(src_new.at[t], src_in.at[t + 1], block_sem.at[t], moved(NEXT))

    def state_copy(t):
        return remote(src_st_new.at[t], src_st_in.at[t + 1], state_sem.at[t], moved(NEXT))

    ends = [
        remote(src_st_new.at[2], src_st_out, end_sem.at[0], moved(SRC_END)),
        remote(src_new.at[2], src_out, end_sem.at[1], moved(SRC_END)),
        remote(dst_st_cur, dst_st_out, end_sem.at[2], moved(DST_END)),
        remote(dst_cur, dst_out, end_sem.at[3], moved(DST_END)),
    ]

    def gather_relations(row_of):
        @pl.loop(0, 32)
        def _(i):
            for j in range(8):
                e = i * 8 + j
                rel_vec[pl.ds(e, 1), :] = table[pl.ds(row_of(e), 1), :]

    def add_third(t, c):
        v = jnp.concatenate(
            [v_own[t, c], v_sib[t, c]], axis=0
        )
        rhs = split(v, axis=1)
        r = jnp.concatenate([idx[t, 2:3, :], idx_sib[t, 2:3, :]], axis=1)
        at = jnp.where(((r >> 7) & 1) == me["core"], positions(r, c), -1)

        @pl.loop(0, 4)
        def _(ch):
            rows = pl.ds(pl.multiple_of(ch * 256, 256), 256)
            hot = one_hot(lax.broadcasted_iota(I32, (256, 512), 0) + ch * 256 == at)
            both = dot(hot, rhs)
            half[c, rows, :] += both[:, :128] + both[:, 128:]

    def work(t, send_values, send_src):
        rows = idx[t]
        columns = jnp.transpose(rows.astype(F32)).astype(I32)
        s_col, d_col, n_col = columns[:, 0:1], columns[:, 1:2], columns[:, 3:4]
        live = columns[:, 4:5].astype(F32)
        lanes = lax.broadcasted_iota(I32, (256, 256), 1) & 127
        src_blk, dst_blk = src_in[t], dst_cur[...]
        dst_two = split(dst_blk)
        src_vec = dot(one_hot(lanes == s_col), split(src_blk))
        dst_vec = dot(one_hot(lanes == d_col), dst_two)
        negb = dot(one_hot(lanes[:, :128] == n_col), dst_two[:128]).astype(BF16)
        rel = rel_vec[...]
        a = src_vec * rel
        ab = a.astype(BF16)
        pos = jnp.sum(a * dst_vec, axis=1, keepdims=True)
        gpos = -sigmoid(-pos) * live
        negs_part, rows_part = [], []
        for c in range(2):
            block = slice(c * 128, (c + 1) * 128)
            neg = dot_nt(ab[block], negb[block])
            gneg = sigmoid(neg) * (1.0 / 128) * live[block]
            negs_part.append(dot(gneg.astype(BF16), negb[block]))
            rows_part.append(dot(jnp.transpose(gneg).astype(BF16), ab[block]))
        gprod = gpos * dst_vec + jnp.concatenate(negs_part, axis=0)
        v = gprod * src_vec
        for c in range(3):
            v_own[t, c] = v[:, c * 128 : (c + 1) * 128]
        send_values()
        subl = lax.broadcasted_iota(I32, (128, 256), 0)
        s_hot = one_hot(subl == rows[0:1])
        grad_src = dot(jnp.concatenate([s_hot, s_hot], axis=1), split(gprod * rel))
        block, state = adagrad(src_blk, src_st_in[t], grad_src)
        src_new[t] = block
        src_st_new[t] = state

        send_src()
        d_hot = one_hot(subl == rows[1:2])
        n_hot = one_hot(subl == rows[3:4])
        grad_dst = dot(
            jnp.concatenate([d_hot, d_hot, n_hot, n_hot], axis=1),
            jnp.concatenate([split(gpos * a), split(jnp.concatenate(rows_part, axis=0))], axis=0),
        )
        block, state = adagrad(dst_blk, dst_st_cur[...], grad_dst)
        dst_cur[...] = block
        dst_st_cur[...] = state

    def enter():
        pl.semaphore_wait(barrier, 28)

    def first_sends():
        enter()
        state_copy(0).start()
        block_copy(0).start()
        pack(1)
        pack(2)
        edge_copy(1, EDGES_1).start()
        edge_copy(2, EDGES_2).start()
        sib_idx_copy(0).start()
        send_v(0)
        half[...] = jnp.zeros_like(half)

    gather_relations(lambda e: r_smem[0, 0, e])
    work(0, lambda: None, first_sends)

    @pl.loop(1, STEPS)
    def _(t):
        edge_copy(t, EDGES_1).wait()
        sib_idx_copy(t).start()
        load = pltpu.make_async_copy(idx.at[t], idx_smem.at[t], smem_sem)
        load.start()
        load.wait()
        gather_relations(lambda e: idx_smem[t, 2, e])
        state_copy(t - 1).wait()
        block_copy(t - 1).wait()

        def send_src():
            @pl.when(t < 2)
            def _():
                state_copy(t).start()
                block_copy(t).start()
                send_v(t)

            @pl.when(t == 2)
            def _():
                ends[0].start()
                ends[1].start()

        def send_values():
            @pl.when(t == 2)
            def _():
                send_v(t)

        work(t, send_values, send_src)

        @pl.when(t == 2)
        def _():
            ends[2].start()
            ends[3].start()

        sib_idx_copy(t - 1).wait()
        for c in THIRDS:
            v_copy(t - 1, c).wait()
            add_third(t - 1, c)

    ahead, across, behind = (lax.rem(me["x"] + o, 4) for o in (1, 2, 3))

    def x_copy(c, k):
        lower, upper = 0, 128
        chunk, first, target, step = (
            (across, lower, relay_in.at[c, 0], 1),
            (across, upper, relay_in.at[c, 1], 3),
            (ahead, upper, near_in.at[c, 0], 1),
            (behind, lower, near_in.at[c, 1], 3),
            (ahead, lower, near_in.at[c, 2], 1),
            (behind, upper, near_in.at[c, 3], 3),
        )[k]
        source = half.at[c, pl.ds(pl.multiple_of(chunk * 256 + first, 128), 128)]
        return remote(source, target, x_sem.at[c, k], partner(me, "x", step))

    z_at = [lax.rem(me["z"] + o, 8) for o in range(8)]

    def z_rows(chunk, first, count):
        return pl.ds(pl.multiple_of(z_at[chunk] * 128 + first, count), count)

    def z_copy(k):
        chunk, first, count, target, step = (
            (3, 0, 128, z_relay.at[0], 1),
            (5, 0, 128, z_relay.at[1], 7),
            (4, 0, 64, z_part.at[0], 2),
            (4, 64, 64, z_part.at[1], 6),
            (1, 0, 128, z_near.at[0], 1),
            (7, 0, 128, z_near.at[1], 7),
            (2, 0, 128, z_near.at[2], 2),
            (6, 0, 128, z_near.at[3], 6),
        )[k]
        return remote(
            half.at[0, z_rows(chunk, first, count)], target, z_sem.at[k], partner(me, "z", step)
        )

    def ring_rows(c, p, j):
        if p == 1:
            return pl.ds(pl.multiple_of(lax.div(j, 2) * 8, 8), 8)
        return pl.ds(pl.multiple_of(j * ring_count(c, p), ring_count(c, p)), ring_count(c, p))

    def ring_count(c, p):
        return 8 if p else 1024 // SIZE[ORDERS[c][0]] // SIZE[ORDERS[c][1]]

    def ring_in(c, p):
        return recv[p].at[c, 0 : SIZE[ORDERS[c][p + 1]] - 1, 0 : ring_count(c, p)]

    def ring_start(c, p):
        axis = ORDERS[c][p + 1]
        for o in range(1, SIZE[axis]):
            target = lax.rem(me[axis] + o, SIZE[axis])
            pltpu.make_async_remote_copy(
                held[p].at[c, ring_rows(c, p, target)],
                ring_in(c, p).at[o - 1],
                ring_sem.at[c, p, 0],
                ring_sem.at[c, p, 1],
                device_id=partner(me, axis, o),
                device_id_type=MESH,
            ).start()

    def ring_all(c, p):
        return remote(ring_in(c, p), ring_in(c, p), ring_sem.at[c, p], sibling)

    def ring_finish(c, p):
        axis = ORDERS[c][p + 1]
        ring_all(c, p).wait_recv()
        total = held[p][c, ring_rows(c, p, me[axis]), :]
        count = total.shape[0]
        for o in range(SIZE[axis] - 1):
            total = total + recv[p][c, o, 0:count]
        return total

    sib_idx_copy(2).wait()
    for c in THIRDS:
        v_copy(2, c).wait()
        add_third(2, c)
        if c == 0:
            for k in range(6):
                z_copy(k).start()
        else:
            for k in range(4):
                x_copy(c, k).start()

    def relay_x(c):
        for k, chunk, first in ((0, ahead, 0), (1, behind, 128)):
            x_copy(c, k).wait_recv()
            rows = pl.ds(pl.multiple_of(chunk * 256 + first, 128), 128)
            half[c, rows, :] += relay_in[c, k]
            x_copy(c, 4 + k).start()

    def relay_z():
        for k, chunk, first in ((0, 2, 0), (1, 6, 64)):
            z_copy(k).wait_recv()
            half[0, z_rows(chunk, 0, 128), :] += z_relay[k]
            z_copy(2 + k).wait_recv()
            half[0, z_rows(chunk, first, 64), :] += z_part[k]
            z_copy(6 + k).start()

    relay_x(2)
    relay_z()
    relay_x(1)
    own = pl.multiple_of(me["x"] * 256, 256)

    def finish_x(c):
        for k in range(2, 6):
            x_copy(c, k).wait_recv()
        held[0][c, 0:128, :] = half[c, pl.ds(own, 128), :] + near_in[c, 1] + near_in[c, 2]
        held[0][c, 128:256, :] = (
            half[c, pl.ds(pl.multiple_of(own + 128, 128), 128), :] + near_in[c, 0] + near_in[c, 3]
        )
        ring_start(c, 0)

    def finish_z():
        for k in range(4, 8):
            z_copy(k).wait_recv()
        total = half[0, z_rows(0, 0, 128), :]
        for k in range(4):
            total = total + z_near[k]
        held[0][0, 0:128, :] = total
        ring_start(0, 0)

    finish_x(2)
    finish_z()
    finish_x(1)
    for c in (2, 0, 1):
        total = ring_finish(c, 0)
        held[1][c, 0 : total.shape[0], :] = total
        ring_start(c, 1)
    last = {}
    for c in (2, 0, 1):
        total = ring_finish(c, 1)
        odd = lax.rem(me[ORDERS[c][2]], 2)
        last[c] = jnp.where(odd == 0, total[0:4], total[4:8])
    grad = jnp.concatenate([last[0], last[1], last[2]], axis=1)
    owner = lax.axis_index("src") * 32 + lax.axis_index("dst")
    near = table[pl.ds(pl.multiple_of(lax.div(owner, 2) * 8, 8), 8), :]
    own_rel = jnp.where(lax.rem(owner, 2) == 0, near[0:4], near[4:8])
    state = as_column(rel_st[...]) + jnp.sum(grad * grad, axis=1, keepdims=True) * (1.0 / 384)
    rel_st_out[...] = as_row(state)
    rel_out[...] = own_rel - 0.1 * grad / jnp.sqrt(state)
    for k in range(8):
        z_copy(k).wait_send()
    for c in ALONG_X:
        for k in range(6):
            x_copy(c, k).wait_send()
    for c in THIRDS:
        for p in range(2):
            ring_all(c, p).wait_send()
    for copy in ends:
        copy.wait()


def store_kernel(*refs):
    sources, targets, held, sems = refs[:6], refs[6:12], refs[12:18], refs[18]
    parts = [(i, slice(j * 32, j * 32 + 32)) for j in range(4) for i in (0, 2)]
    parts += [(i, slice(None)) for i in (1, 3, 4, 5)]
    loads = [
        pltpu.make_async_copy(sources[i].at[rows], held[i].at[rows], sems.at[0, n])
        for n, (i, rows) in enumerate(parts)
    ]
    stores = [
        pltpu.make_async_copy(held[i].at[rows], targets[i].at[rows], sems.at[1, n])
        for n, (i, rows) in enumerate(parts)
    ]
    for load in loads:
        load.start()
    for load, store in zip(loads, stores):
        load.wait()
        store.start()
    for store in stores:
        store.wait()


def on_device(
    source_embedding_table,
    source_adagrad_state,
    destination_embedding_table,
    destination_adagrad_state,
    relations,
    rel_state,
    source_edge_rows,
    destination_edge_rows,
    edge_relation_index,
    negative_block_rows,
    bucket_block_counts,
):
    vmem, hbm = pl.BlockSpec(memory_space=pltpu.VMEM), pl.BlockSpec(memory_space=pl.ANY)
    dma = pltpu.SemaphoreType.DMA
    scratch = [
        pltpu.VMEM((2048, 384), F32),
        pltpu.VMEM((1, 4), F32),
        pltpu.VMEM((3, 1, 256), I32),
        pltpu.VMEM((3, 1, 256), I32),
        pltpu.VMEM((3, 1, 256), I32),
        pltpu.VMEM((3, 2, 128), I32),
        pltpu.SMEM((3, 1, 256), I32),
        pltpu.SMEM((1, 3), I32),
        pltpu.VMEM((3, 8, 256), I32),
        pltpu.VMEM((3, 8, 256), I32),
        pltpu.VMEM((3, 8, 256), I32),
        pltpu.SMEM((3, 8, 256), I32),
        pltpu.VMEM((3, 128, 384), F32),
        pltpu.VMEM((3, 1, 128), F32),
        pltpu.VMEM((3, 128, 384), F32),
        pltpu.VMEM((3, 1, 128), F32),
        pltpu.VMEM((128, 384), F32),
        pltpu.VMEM((1, 128), F32),
        pltpu.VMEM((256, 384), F32),
        pltpu.VMEM((3, 3, 256, 128), F32),
        pltpu.VMEM((3, 3, 256, 128), F32),
        pltpu.VMEM((3, 1024, 128), F32),
    ]
    scratch += [
        pltpu.VMEM((3, 2, 128, 128), F32),
        pltpu.VMEM((3, 4, 128, 128), F32),
        pltpu.VMEM((3, 7, 32, 128), F32),
        pltpu.VMEM((3, 7, 8, 128), F32),
        pltpu.VMEM((3, 256, 128), F32),
        pltpu.VMEM((3, 32, 128), F32),
        pltpu.VMEM((2, 128, 128), F32),
        pltpu.VMEM((2, 64, 128), F32),
        pltpu.VMEM((4, 128, 128), F32),
    ]
    scratch += [dma((12,)), dma, dma((3, 2)), dma((3, 2)), dma((2, 2)), dma((2, 2)), dma((3, 3, 2)), dma((4, 2))]
    scratch += [dma((3, 6, 2)), dma((8, 2)), dma((3, 2, 2))]
    block = jax.ShapeDtypeStruct((128, 384), F32)
    row = jax.ShapeDtypeStruct((1, 128), F32)
    results = (block, row, block, row)
    results += (jax.ShapeDtypeStruct((4, 384), F32), jax.ShapeDtypeStruct((1, 4), F32))
    outs = pl.pallas_call(
        window_kernel,
        out_shape=results,
        in_specs=[hbm] * 11,
        out_specs=(hbm,) * 4 + (vmem,) * 2,
        scratch_shapes=scratch,
        compiler_params=pltpu.CompilerParams(
            collective_id=0, has_side_effects=True, vmem_limit_bytes=VMEM_LIMIT
        ),
    )(
        source_embedding_table[0, 0],
        source_adagrad_state[0],
        destination_embedding_table[0, 0],
        destination_adagrad_state[0],
        relations,
        rel_state[None],
        source_edge_rows.reshape(STEPS, 1, 256),
        destination_edge_rows.reshape(STEPS, 1, 256),
        edge_relation_index.reshape(STEPS, 1, 256),
        negative_block_rows[0, 0],
        bucket_block_counts[0],
    )
    src_out, src_st, dst_out, dst_st, rel_out, rel_st = pl.pallas_call(
        store_kernel,
        out_shape=results,
        in_specs=[hbm] * 6,
        out_specs=(hbm,) * 6,
        scratch_shapes=[pltpu.VMEM(r.shape, F32) for r in results] + [dma((2, 12))],
        compiler_params=pltpu.CompilerParams(vmem_limit_bytes=VMEM_LIMIT),
    )(*outs)
    return (
        src_out[None, None],
        src_st[None],
        dst_out[None, None],
        dst_st[None],
        rel_out,
        rel_st[0],
    )


def solution(mesh):
    in_specs = (
        P("src", "dst", None, None),
        P("src", "dst", None),
        P("src", "dst", None, None),
        P("src", "dst", None),
        P(),
        P(("src", "dst")),
        P("src", "dst", None, None),
        P("src", "dst", None, None),
        P("src", "dst", None, None),
        P("src", "dst", None, None, None),
        P("src", "dst", None),
    )
    out_specs = (
        P("src", "dst", None, None),
        P("src", "dst", None),
        P("src", "dst", None, None),
        P("src", "dst", None),
        P(("src", "dst"), None),
        P(("src", "dst")),
    )
    return jax.shard_map(
        on_device, mesh=mesh, in_specs=in_specs, out_specs=out_specs, check_vma=False
    )
```
